128 devices in a mesh: occ: 8 (over y, core), vir: 16 (over z, x).
Axes of the slice: x: 4, y: 4, z: 4, core: 2. Of those that a mesh axis runs over, the one named last changes fastest.
Arguments:
- amplitudes: bfloat16 [8, 2, 4096, 4096], P('occ', None, 'vir'), may hold values from -6 to 6
- ladder_ints: bfloat16 [2, 16, 3, 256, 256], P(None, 'vir'), may hold values from -0.21875 to 0.21875
- tile_cols: int32 [16, 3], replicated, may hold values from 0 to 15, as said below
- tile_counts: int32 [16], replicated, may hold values from 1 to 3, as said below
- cycle_ints: bfloat16 [2, 8, 4096], P(None, 'occ', 'vir'), may hold values from -0.375 to 0.375
Outputs:
- residual: bfloat16 [8, 2, 4096, 4096], P('occ', None, 'vir')
The draws below stay inside these ranges and needn't reach their ends.
Inputs may be any that keep to these rules, and one draw needn't show every extreme that they name: `tile_cols`: in tile row X, slot 0 holds X itself and the 3 slots hold distinct tiles. `tile_counts`: some tile row uses all 3 slots.
All inputs are finite; a program needn't handle non-finite values.
Results may differ from the reference program's by a relative error of at most 0.009.
Values may be sent and summed in bfloat16 or wider, within the bound.
No kernel may reach another device: no remote copies, remote signals or barrier semaphores. Data moves between devices by JAX's collectives and lax.ppermute only.
A program may use at most 192 MiB of HBM per device.

```python
import jax
import jax.numpy as jnp
from jax import lax

TILE = 256
KMAX = 3
NQ = 2
JW = 2
NT = 16
NV = 4096
O = 8


def draw_tile_cols(key, part):
    key = jax.random.fold_in(key, 11)
    scores = jax.random.randint(key, (NT, NT), 0, 1024) * NT + jnp.arange(NT)[None, :]
    scores = jnp.where(jnp.eye(NT, dtype=bool), -1, scores)
    ranking = jnp.argsort(scores, axis=1, stable=True)
    return ranking[:, :KMAX].astype(jnp.int32)


def draw_tile_counts(key, part):
    key = jax.random.fold_in(key, 12)
    key_counts, key_full = jax.random.split(key)
    counts = jax.random.randint(key_counts, (NT,), 1, KMAX + 1)
    full_row = jax.random.randint(key_full, (), 0, NT)
    return jnp.where(jnp.arange(NT) == full_row, KMAX, counts).astype(jnp.int32)


def levels(own_key, shape, cuts, low, top_value):
    def one(dim, parts):
        heights = jax.random.uniform(jax.random.fold_in(jax.random.fold_in(own_key, 6), dim), (parts,), jnp.float32, low / len(cuts), top_value / len(cuts))
        return jnp.repeat(jnp.exp(heights), shape[dim] // parts).reshape((-1,) + (1,) * (len(shape) - dim - 1))

    loudness = one(*cuts[0])
    for cut in cuts[1:]:
        loudness = loudness * one(*cut)
    return loudness


def normal_values(stream_key, dims, width, limit, cuts=(), held_as=jnp.bfloat16):
    result = width * jax.random.normal(stream_key, dims, jnp.float32)
    if cuts:
        result = result * levels(stream_key, dims, cuts, -0.22, 0.18)
    return jnp.clip(result, -limit, limit).astype(held_as)


def setup_inputs(seed: int = 0) -> dict:
    seeds = jax.random.split(jax.random.key(seed), 6)
    return {
        "amplitudes": normal_values(seeds[0], (O, JW, NV, NV), 1.0, 6.0, ((0, 8), (2, 16))),
        "ladder_ints": normal_values(seeds[1], (NQ, NT, KMAX, TILE, TILE), (KMAX * TILE) ** -0.5, 0.21875, ((1, 16),)),
        "tile_cols": draw_tile_cols(jax.random.fold_in(seeds[5], 71), 0),
        "tile_counts": draw_tile_counts(jax.random.fold_in(seeds[5], 71), 0),
        "cycle_ints": normal_values(seeds[4], (NQ, O, NV), TILE ** -0.5, 0.375, ((1, 8), (2, 16))),
    }


def reference(amplitudes, ladder_ints, tile_cols, tile_counts, cycle_ints):
    aux_count, tile_count, slot_count, tile_rows, _ = ladder_ints.shape
    virtuals = amplitudes.shape[2]
    partners = amplitudes.shape[1]
    live_slots = (lax.broadcasted_iota(jnp.int32, (tile_count, slot_count), 1) < tile_counts[:, None]).astype(ladder_ints.dtype)
    int_tiles = ladder_ints * live_slots[None, :, :, None, None]
    cycle_swapped = jnp.swapaxes(cycle_ints, 0, 1)

    def cycle_step(total, pieces):
        amp_one, cycle_one = pieces
        total = total + jnp.einsum("qc,jcb->qjb", cycle_one.astype(jnp.float32), amp_one.astype(jnp.float32))
        return total, None

    cycle_inter, _ = lax.scan(cycle_step, jnp.zeros((aux_count, partners, virtuals), jnp.float32), (amplitudes, cycle_swapped))

    def one_orbital(pieces):
        amp_one, cycle_one = pieces
        stacked = amp_one.reshape(partners, tile_count, tile_rows, virtuals)
        total = jnp.zeros((aux_count, partners, tile_count, tile_rows, virtuals), jnp.float32)
        for slot_index in range(slot_count):
            chosen = jnp.take(stacked, tile_cols[:, slot_index], axis=1)
            total = total + jnp.einsum("qaxc,jacd->qjaxd", int_tiles[:, :, slot_index].astype(jnp.float32), chosen.astype(jnp.float32))
        half_done = total.astype(jnp.bfloat16).reshape(aux_count, partners, virtuals, tile_count, tile_rows)
        ladder = jnp.zeros((partners, virtuals, tile_count, tile_rows), jnp.float32)
        for slot_index in range(slot_count):
            picked = jnp.take(half_done, tile_cols[:, slot_index], axis=3)
            ladder = ladder + jnp.einsum("qjaby,qbxy->jabx", picked.astype(jnp.float32), int_tiles[:, :, slot_index].astype(jnp.float32))
        cycle_term = jnp.einsum("qa,qjb->jab", cycle_one.astype(jnp.float32), cycle_inter)
        return (ladder.reshape(partners, virtuals, virtuals) + cycle_term).astype(jnp.bfloat16)

    return lax.map(one_orbital, (amplitudes, cycle_swapped))
```

```python
import jax
import jax.numpy as jnp
from jax import lax
from jax.experimental import pallas as pl
from jax.experimental.pallas import tpu as pltpu
from jax.sharding import PartitionSpec as P

TILE = 256
SLOTS = 3
AUX = 2
WIDE = 1024
ROWS_PER_STEP = 2


def ladder_kernel(
    partner, parts, cols_ref, counts_ref, own_ref, t0_ref, t1_ref, t2_ref, ints_ref, cycle_ref, left_ref, out_ref, half_ref
):
    tile_count = counts_ref.shape[0]
    step = pl.program_id(0)
    first_steps = tile_count * TILE // WIDE
    per_step = WIDE // TILE

    @pl.when(step < first_steps)
    def _():
        for piece in range(per_step):
            span = slice(piece * TILE, (piece + 1) * TILE)
            total = jnp.dot(own_ref[0], t0_ref[:, span], preferred_element_type=jnp.float32)
            total += jnp.dot(own_ref[1], t1_ref[:, span], preferred_element_type=jnp.float32)
            total += jnp.dot(own_ref[2], t2_ref[:, span], preferred_element_type=jnp.float32)
            half_ref[step * per_step + piece] = total.reshape(AUX, TILE, TILE).astype(jnp.bfloat16)

    @pl.when(step >= first_steps)
    def _():
        part_rows = AUX * SLOTS * TILE // parts
        for piece in range(ROWS_PER_STEP):
            row = (step - first_steps) * ROWS_PER_STEP + piece
            count = counts_ref[row]
            for slots in range(1, SLOTS + 1):

                @pl.when(count == slots)
                def _(slots=slots, piece=piece, row=row):
                    ints = ints_ref[:, piece * part_rows : (piece + 1) * part_rows, :].reshape(AUX * SLOTS * TILE, TILE)
                    total = jnp.zeros((TILE, TILE), jnp.float32)
                    for slot in range(slots):
                        half = half_ref[cols_ref[row * SLOTS + slot]]
                        for aux in range(AUX):
                            at = (aux * SLOTS + slot) * TILE
                            total += lax.dot_general(
                                half[aux],
                                ints[at : at + TILE],
                                (((1,), (1,)), ((), ())),
                                preferred_element_type=jnp.float32,
                            )
                    for aux in range(AUX):
                        line = (aux * 2 + partner) * tile_count + row
                        total += left_ref[:, aux : aux + 1] * cycle_ref[pl.ds(line, 1), :]
                    out_ref[:, piece * TILE : (piece + 1) * TILE] = total.astype(jnp.bfloat16)


def ladder(partner, parts, cols, counts, own, rows, ints, cycle, left):
    tile_count = counts.shape[0]
    first_steps = tile_count * TILE // WIDE
    last_steps = tile_count // ROWS_PER_STEP
    part_rows = AUX * SLOTS * TILE // parts
    row_spec = pl.BlockSpec((TILE, WIDE), lambda g, *_: (0, jnp.minimum(g, first_steps - 1)))
    whole = lambda shape: pl.BlockSpec(shape, lambda g, *_: (0,) * len(shape))
    return pl.pallas_call(
        lambda *refs: ladder_kernel(partner, parts, *refs),
        grid_spec=pltpu.PrefetchScalarGridSpec(
            num_scalar_prefetch=2,
            grid=(first_steps + last_steps,),
            in_specs=[
                whole((SLOTS, AUX * TILE, TILE)),
                row_spec,
                row_spec,
                row_spec,
                pl.BlockSpec((parts, ROWS_PER_STEP * part_rows, TILE), lambda g, *_: (0, jnp.maximum(g - first_steps, 0), 0)),
                whole(cycle.shape),
                whole(left.shape),
            ],
            out_specs=pl.BlockSpec((TILE, ROWS_PER_STEP * TILE), lambda g, *_: (0, jnp.maximum(g - first_steps, 0))),
            scratch_shapes=[pltpu.VMEM((tile_count, AUX, TILE, TILE), jnp.bfloat16)],
        ),
        out_shape=jax.ShapeDtypeStruct((TILE, tile_count * TILE), jnp.bfloat16),
        compiler_params=pltpu.CompilerParams(vmem_limit_bytes=40 * 1024 * 1024),
        cost_estimate=pl.CostEstimate(flops=6 * 10**9, bytes_accessed=20 * 2**20, transcendentals=0),
    )(cols, counts, own, *rows, ints, cycle, left)


def body(amplitudes, ladder_ints, tile_cols, tile_counts, cycle_ints):
    tile_count = tile_cols.shape[0]
    partners = amplitudes.shape[1]
    virtuals = amplitudes.shape[3]
    parts = lax.axis_size("occ")
    amps = amplitudes[0]

    part_rows = AUX * SLOTS * TILE // parts
    flat_ints = ladder_ints.reshape(AUX * SLOTS * TILE, TILE)
    own_part = lax.dynamic_slice_in_dim(flat_ints, lax.axis_index("occ") * part_rows, part_rows, axis=0)
    left = cycle_ints[:, 0, :]
    cycle_local = jnp.einsum("qc,jcb->qjb", left, amps, preferred_element_type=jnp.float32)
    lines = AUX * partners * tile_count
    payload = jnp.concatenate([own_part, cycle_local.astype(jnp.bfloat16).reshape(lines, TILE)])
    over_vir = lax.all_gather(payload, "vir", axis=0)
    cycle_vir = jnp.sum(over_vir[:, part_rows:].astype(jnp.float32), axis=0).astype(jnp.bfloat16)
    payload = jnp.concatenate([over_vir[:, :part_rows].reshape(tile_count * part_rows, TILE), cycle_vir])
    ints = lax.all_gather(payload, "occ", axis=0)
    cycle = jnp.sum(ints[:, tile_count * part_rows :].astype(jnp.float32), axis=0)

    me = lax.axis_index("vir")
    live = (jnp.arange(SLOTS) < tile_counts[me]).astype(jnp.bfloat16)
    own = (ladder_ints[:, 0] * live[None, :, None, None]).transpose(1, 0, 2, 3).reshape(SLOTS, AUX * TILE, TILE)

    cols = tile_cols.reshape(-1)
    left = left.astype(jnp.float32).T

    spread = []
    for partner in range(partners):
        chunks = amps[partner].reshape(tile_count, TILE // tile_count, virtuals)
        spread.append(lax.all_to_all(chunks, "vir", split_axis=0, concat_axis=0, tiled=True))
    outs = []
    for partner in range(partners):
        rows = [amps[partner]]
        for slot in range(1, SLOTS):
            picked = jnp.take(spread[partner], tile_cols[:, slot], axis=0, mode="clip")
            fetched = lax.all_to_all(picked, "vir", split_axis=0, concat_axis=0, tiled=True)
            rows.append(fetched.reshape(TILE, virtuals))
        outs.append(ladder(partner, parts, cols, tile_counts, own, rows, ints, cycle, left))
    return jnp.stack(outs)[None]


def solution(mesh):
    in_specs = (
        P("occ", None, "vir", None),
        P(None, "vir", None, None, None),
        P(),
        P(),
        P(None, "occ", "vir"),
    )
    out_specs = P("occ", None, "vir", None)
    return jax.shard_map(body, mesh=mesh, in_specs=in_specs, out_specs=out_specs, check_vma=False)
```

```python
import functools

import jax
import jax.numpy as jnp
from jax import lax
from jax.experimental import pallas as pl
from jax.experimental.pallas import tpu as pltpu
from jax.sharding import PartitionSpec as P

ROW_CHUNKS = 4
INT_CHUNKS = 8
EXTRA = 16
MIB = 2**20
HBM = pl.BlockSpec(memory_space=pltpu.HBM)
VMEM = pl.BlockSpec(memory_space=pltpu.VMEM)
SMEM = pl.BlockSpec(memory_space=pltpu.SMEM)


def pairs(total, count):
    values = total[..., :count, :]
    rest = values - values.astype(jnp.bfloat16).astype(jnp.float32)
    empty = jnp.zeros(values.shape[:-2] + (EXTRA - 2 * count, values.shape[-1]), jnp.float32)
    return jnp.concatenate([values, rest, empty], axis=-2).astype(jnp.bfloat16)


def stage_kernel(
    place_ref,
    counts_ref,
    cols_ref,
    amps_hbm,
    own_ints_ref,
    left_ref,
    chunks_hbm,
    held_ref,
    total_ref,
    extra_ref,
    part_ref,
    in_sems,
    out_sems,
    extra_sem,
    part_sems,
):
    partners, chunk_count, chunk_rows, virtuals = amps_hbm.shape
    aux_count, slot_count, tile, _ = own_ints_ref.shape
    columns = virtuals // tile
    lines = aux_count * partners
    part = part_ref.shape[0] // (aux_count * slot_count)
    loads = [pltpu.make_async_copy(amps_hbm.at[index], held_ref.at[index], in_sems.at[index]) for index in range(partners)]

    def store(index, column):
        span = pl.ds(column * tile, tile)
        lines = pl.ds((index * columns + column) * chunk_rows, chunk_rows)
        return pltpu.make_async_copy(
            held_ref.at[index, :, :, span], chunks_hbm.at[:, lines, :], out_sems.at[index, column]
        )

    for load in loads:
        load.start()

    count = counts_ref[place_ref[0]]
    first = pl.multiple_of(place_ref[1] * part, part)
    for aux in range(aux_count):
        for slot in range(slot_count):
            live = (slot < count).astype(jnp.float32).astype(jnp.bfloat16)
            at = (aux * slot_count + slot) * part
            part_ref[at : at + part, :] = own_ints_ref[aux, slot, pl.ds(first, part), :] * live

    def send(chunk):
        lines = pl.ds(partners * tile + EXTRA, part_ref.shape[0])
        return pltpu.make_async_copy(part_ref, chunks_hbm.at[chunk, lines, :], part_sems.at[chunk])

    for chunk in range(chunk_count):
        send(chunk).start()

    for index in range(partners):
        loads[index].wait()
        for column in range(columns):
            store(index, column).start()
        for column in range(columns):
            rows = held_ref[index, :, :, column * tile : (column + 1) * tile].reshape(tile, tile)
            total = jnp.dot(left_ref[...], rows, preferred_element_type=jnp.float32)
            for aux in range(aux_count):
                line = aux * partners + index
                total_ref[column, line : line + 1, :] = total[aux : aux + 1]
    extra_ref[...] = pairs(total_ref[...], lines)
    extra = pltpu.make_async_copy(extra_ref, chunks_hbm.at[:, pl.ds(partners * tile, EXTRA), :], extra_sem)
    extra.start()
    for index in range(partners):
        for column in range(columns):
            store(index, column).wait()
    extra.wait()
    for chunk in range(chunk_count):
        send(chunk).wait()


def stage(place, counts, cols, amps, own_ints, left, parts):
    partners, chunk_count, chunk_rows, virtuals = amps.shape
    aux_count, slot_count, tile, _ = own_ints.shape
    columns = virtuals // tile
    part_rows = aux_count * slot_count * tile // parts
    return pl.pallas_call(
        stage_kernel,
        in_specs=[SMEM, SMEM, SMEM, HBM, VMEM, VMEM],
        out_specs=HBM,
        out_shape=jax.ShapeDtypeStruct((chunk_count, partners * tile + EXTRA + part_rows, tile), amps.dtype),
        scratch_shapes=[
            pltpu.VMEM(amps.shape, amps.dtype),
            pltpu.VMEM((columns, aux_count * partners, tile), jnp.float32),
            pltpu.VMEM((columns, EXTRA, tile), amps.dtype),
            pltpu.VMEM((part_rows, tile), amps.dtype),
            pltpu.SemaphoreType.DMA((partners,)),
            pltpu.SemaphoreType.DMA((partners, columns)),
            pltpu.SemaphoreType.DMA,
            pltpu.SemaphoreType.DMA((chunk_count,)),
        ],
        compiler_params=pltpu.CompilerParams(vmem_limit_bytes=60 * MIB),
        cost_estimate=pl.CostEstimate(flops=10**7, bytes_accessed=9 * MIB, transcendentals=0),
    )(place, counts, cols, amps, own_ints, left)


def pick_kernel(
    partners, lines, cols_ref, spread_hbm, first_hbm, later_hbm, ints_hbm, first_ref, held_ref, extra_ref, part_ref, in_sems, out_sems, extra_sems
):
    chunks, slots = in_sems.shape[1:]
    tile = held_ref.shape[3]
    part_rows = part_ref.shape[1]

    def fetch(partner, chunk, slot):
        source = spread_hbm.at[cols_ref[slot + 1, chunk], pl.ds(partner * tile, tile), :]
        place = first_ref.at[chunk] if partner == 0 else held_ref.at[partner - 1, chunk]
        return pltpu.make_async_copy(source, place.at[pl.ds(slot * tile, tile), :], in_sems.at[partner, chunk, slot])

    def store(partner, chunk):
        source = first_ref.at[chunk] if partner == 0 else held_ref.at[partner - 1, chunk]
        place = first_hbm.at[chunk] if partner == 0 else later_hbm.at[partner - 1, chunk]
        return pltpu.make_async_copy(source, place, out_sems.at[partner, chunk])

    extra = pltpu.make_async_copy(spread_hbm.at[:, pl.ds(partners * tile, EXTRA), :], extra_ref, extra_sems.at[0])
    part_in = pltpu.make_async_copy(spread_hbm.at[:, pl.ds(partners * tile + EXTRA, part_rows), :], part_ref, extra_sems.at[1])
    part_out = pltpu.make_async_copy(part_ref, ints_hbm, extra_sems.at[2])
    extra.start()
    for partner in range(partners):

        @pl.loop(0, chunks)
        def _(chunk, partner=partner):
            for slot in range(slots):
                fetch(partner, chunk, slot).start()

        if partner == 0:
            part_in.start()

    extra.wait()
    total = jnp.sum(extra_ref[...].astype(jnp.float32), axis=0)
    total = pairs(total[:lines] + total[lines : 2 * lines], lines)
    for chunk in range(chunks):
        first_ref[chunk, slots * tile :, :] = total

    for partner in range(partners):

        @pl.loop(0, chunks)
        def _(chunk, partner=partner):
            for slot in range(slots):
                fetch(partner, chunk, slot).wait()
            store(partner, chunk).start()

        if partner == 0:
            part_in.wait()
            part_out.start()

    for partner in range(partners):

        @pl.loop(0, chunks)
        def _(chunk, partner=partner):
            store(partner, chunk).wait()

    part_out.wait()


def pick(partners, lines, spread, cols):
    slots, chunks = cols.shape
    rows, tile = spread.shape[1:]
    shape = (partners - 1, chunks, (slots - 1) * tile, tile)
    first = (chunks, (slots - 1) * tile + EXTRA, tile)
    part_rows = rows - partners * tile - EXTRA
    return pl.pallas_call(
        functools.partial(pick_kernel, partners, lines),
        in_specs=[SMEM, HBM],
        out_specs=[HBM] * 3,
        out_shape=[
            jax.ShapeDtypeStruct(first, spread.dtype),
            jax.ShapeDtypeStruct(shape, spread.dtype),
            jax.ShapeDtypeStruct((chunks, part_rows, tile), spread.dtype),
        ],
        scratch_shapes=[
            pltpu.VMEM(first, spread.dtype),
            pltpu.VMEM(shape, spread.dtype),
            pltpu.VMEM((chunks, EXTRA, tile), spread.dtype),
            pltpu.VMEM((chunks, part_rows, tile), spread.dtype),
            pltpu.SemaphoreType.DMA((partners, chunks, slots - 1)),
            pltpu.SemaphoreType.DMA((partners, chunks)),
            pltpu.SemaphoreType.DMA((3,)),
        ],
        compiler_params=pltpu.CompilerParams(vmem_limit_bytes=60 * MIB),
        cost_estimate=pl.CostEstimate(flops=0, bytes_accessed=20 * MIB, transcendentals=0),
    )(cols, spread)


def ladder_kernel(
    partner, cols_ref, counts_ref, place_ref, amps_hbm, fetched_hbm, ints_hbm, cycle_ref, own_ints_ref, left_ref, *rest
):
    out_hbm, near_ref, far_ref, ints_ref, sums_ref, own_ref, half_ref, out_ref = rest[-12:-4]
    near_sems, far_sems, int_sems, out_sems = rest[-4:]
    tile_count, tile, _ = half_ref.shape
    aux_count, slot_count = own_ints_ref.shape[:2]
    partners, _, chunk_rows, virtuals = amps_hbm.shape
    wide = virtuals // ROW_CHUNKS
    part_rows = ints_ref.shape[1] // tile_count
    part = part_rows // (aux_count * slot_count)
    group = tile_count // INT_CHUNKS
    per_chunk = wide // tile

    def near_copy(chunk):
        span = pl.ds(pl.multiple_of(chunk * wide, wide), wide)
        return pltpu.make_async_copy(amps_hbm.at[partner, :, :, span], near_ref.at[:, :, span], near_sems.at[chunk])

    def far_copy(slot, chunk):
        lines = per_chunk * chunk_rows
        first = pl.multiple_of(slot * tile + chunk * lines, lines)
        return pltpu.make_async_copy(
            fetched_hbm.at[:, pl.ds(first, lines), :], far_ref.at[:, pl.ds(first, lines), :], far_sems.at[slot, chunk]
        )

    def int_copy(chunk):
        lines = group * part_rows
        span = pl.ds(pl.multiple_of(chunk * lines, lines), lines)
        return pltpu.make_async_copy(ints_hbm.at[:, span, :], ints_ref.at[:, span, :], int_sems.at[chunk])

    def out_copy(chunk):
        span = pl.ds(pl.multiple_of(chunk * group * tile, group * tile), group * tile)
        return pltpu.make_async_copy(out_ref.at[:, span], out_hbm.at[partner, :, span], out_sems.at[chunk])

    for chunk in range(ROW_CHUNKS):
        near_copy(chunk).start()
        for slot in range(slot_count - 1):
            far_copy(slot, chunk).start()
    for chunk in range(INT_CHUNKS):
        int_copy(chunk).start()

    count = counts_ref[place_ref[0]]
    for aux in range(aux_count):
        for slot in range(slot_count):
            live = (slot < count).astype(jnp.float32).astype(jnp.bfloat16)
            own_ref[aux * tile : (aux + 1) * tile, slot * tile : (slot + 1) * tile] = own_ints_ref[aux, slot] * live
    lines = aux_count * partners
    sums = jnp.sum(cycle_ref[...].astype(jnp.float32), axis=0)
    sums_ref[...] = sums[:, :lines] + sums[:, lines : 2 * lines]
    line = lax.broadcasted_iota(jnp.int32, (8, tile), 0)
    left = jnp.zeros((8, tile), jnp.float32)
    for aux in range(aux_count):
        left = jnp.where(line == aux, left_ref[aux : aux + 1, :].astype(jnp.float32), left)
    left = left.T

    @pl.loop(0, ROW_CHUNKS)
    def _(chunk):
        near_copy(chunk).wait()
        for slot in range(slot_count - 1):
            far_copy(slot, chunk).wait()
        for piece in range(per_chunk):
            column = chunk * per_chunk + piece
            span = pl.ds(pl.multiple_of(column * tile, tile), tile)
            rows = [near_ref[:, :, span].reshape(tile, tile)]
            for slot in range(slot_count - 1):
                first = pl.multiple_of(slot * tile + column * chunk_rows, chunk_rows)
                rows.append(far_ref[:, pl.ds(first, chunk_rows), :].reshape(tile, tile))
            total = jnp.dot(own_ref[...], jnp.concatenate(rows), preferred_element_type=jnp.float32).astype(jnp.bfloat16)
            for aux in range(aux_count):
                half_ref[column, :, aux * tile : (aux + 1) * tile] = total[aux * tile : (aux + 1) * tile]

    @pl.loop(0, INT_CHUNKS)
    def _(chunk):
        int_copy(chunk).wait()
        for piece in range(group):
            row = chunk * group + piece
            halves, ints = [], []
            for slot in range(slot_count):
                halves.append(half_ref[cols_ref[slot, row]])
                for aux in range(aux_count):
                    first = pl.multiple_of(row * part_rows + (aux * slot_count + slot) * part, part)
                    ints.append(ints_ref[:, pl.ds(first, part), :].reshape(tile, tile))
            total = lax.dot_general(
                jnp.concatenate(halves, axis=1),
                jnp.concatenate(ints, axis=1),
                (((1,), (1,)), ((), ())),
                preferred_element_type=jnp.float32,
            )
            for aux in range(aux_count):
                line = aux * partners + partner
                total += left[:, aux : aux + 1] * sums_ref[row, line : line + 1, :]
            out_ref[:, pl.ds(pl.multiple_of(row * tile, tile), tile)] = total.astype(jnp.bfloat16)
        out_copy(chunk).start()

    @pl.loop(0, INT_CHUNKS)
    def _(chunk):
        out_copy(chunk).wait()


def ladder(partner, cols, counts, place, amps, fetched, ints, cycle, own_ints, left, before):
    partners, chunks, chunk_rows, virtuals = amps.shape
    aux_count, slot_count, tile, _ = own_ints.shape
    tile_count = virtuals // tile
    args = [cols, counts, place, amps, fetched, ints, cycle, own_ints, left]
    specs = [SMEM] * 3 + [HBM] * 3 + [VMEM] * 3
    aliases = {}
    if before is not None:
        aliases = {len(args): 0}
        args.append(before)
        specs.append(HBM)
    return pl.pallas_call(
        functools.partial(ladder_kernel, partner),
        in_specs=specs,
        out_specs=HBM,
        out_shape=jax.ShapeDtypeStruct((partners, tile, virtuals), jnp.bfloat16),
        input_output_aliases=aliases,
        scratch_shapes=[
            pltpu.VMEM((chunks, chunk_rows, virtuals), jnp.bfloat16),
            pltpu.VMEM((chunks, (slot_count - 1) * tile, tile), jnp.bfloat16),
            pltpu.VMEM(ints.shape, jnp.bfloat16),
            pltpu.VMEM((tile_count, aux_count * partners, tile), jnp.float32),
            pltpu.VMEM((aux_count * tile, slot_count * tile), jnp.bfloat16),
            pltpu.VMEM((tile_count, tile, aux_count * tile), jnp.bfloat16),
            pltpu.VMEM((tile, virtuals), jnp.bfloat16),
            pltpu.SemaphoreType.DMA((ROW_CHUNKS,)),
            pltpu.SemaphoreType.DMA((slot_count - 1, ROW_CHUNKS)),
            pltpu.SemaphoreType.DMA((INT_CHUNKS,)),
            pltpu.SemaphoreType.DMA((INT_CHUNKS,)),
        ],
        compiler_params=pltpu.CompilerParams(vmem_limit_bytes=60 * MIB),
        cost_estimate=pl.CostEstimate(flops=6 * 10**9, bytes_accessed=20 * MIB, transcendentals=0),
    )(*args)


def cut_kernel(first, source_hbm, after_hbm, out_ref, sem):
    copy = pltpu.make_async_copy(source_hbm.at[:, pl.ds(first, out_ref.shape[1]), :], out_ref, sem)
    copy.start()
    copy.wait()


def cut(source, first, rows, after):
    chunks, _, width = source.shape
    return pl.pallas_call(
        functools.partial(cut_kernel, first),
        in_specs=[HBM, HBM],
        out_specs=VMEM,
        out_shape=jax.ShapeDtypeStruct((chunks, rows, width), source.dtype),
        scratch_shapes=[pltpu.SemaphoreType.DMA],
        compiler_params=pltpu.CompilerParams(vmem_limit_bytes=60 * MIB),
        cost_estimate=pl.CostEstimate(flops=0, bytes_accessed=2 * MIB, transcendentals=0),
    )(source, after)


def body(amplitudes, ladder_ints, tile_cols, tile_counts, cycle_ints):
    tile_count, slot_count = tile_cols.shape
    aux_count = ladder_ints.shape[0]
    tile = ladder_ints.shape[3]
    partners = amplitudes.shape[1]
    virtuals = amplitudes.shape[3]
    parts = lax.axis_size("occ")
    chunked = amplitudes[0].reshape(partners, tile_count, tile // tile_count, virtuals)
    own_ints = ladder_ints[:, 0]
    left = cycle_ints[:, 0, :]
    place = jnp.stack([lax.axis_index("vir"), lax.axis_index("occ")])
    lines = aux_count * partners
    cols = tile_cols.T

    chunks = stage(place, tile_counts, cols, chunked, own_ints, left, parts)
    spread = lax.all_to_all(chunks, "vir", split_axis=0, concat_axis=0, tiled=True)
    first, later, here = pick(partners, lines, spread, cols)
    picked = [first] + [later[index] for index in range(partners - 1)]

    ints = lax.all_gather(here, "occ", axis=0).reshape(parts, -1, tile)

    out = None
    for partner in range(partners):
        fetched = lax.all_to_all(picked[partner], "vir", split_axis=0, concat_axis=0, tiled=True)
        if partner == 0:
            sums = cut(fetched, (slot_count - 1) * tile, EXTRA, ints)
            cycle = lax.all_gather(sums, "occ", axis=0)
        out = ladder(partner, cols, tile_counts, place, chunked, fetched, ints, cycle, own_ints, left, out)
    return out[None]


def solution(mesh):
    in_specs = (
        P("occ", None, "vir", None),
        P(None, "vir", None, None, None),
        P(),
        P(),
        P(None, "occ", "vir"),
    )
    out_specs = P("occ", None, "vir", None)
    return jax.shard_map(body, mesh=mesh, in_specs=in_specs, out_specs=out_specs, check_vma=False)
```

```python
import functools

import jax
import jax.numpy as jnp
from jax import lax
from jax.experimental import pallas as pl
from jax.experimental.pallas import tpu as pltpu
from jax.sharding import PartitionSpec as P

ROW_CHUNKS = 4
INT_CHUNKS = 4
MIB = 2**20
HBM = pl.BlockSpec(memory_space=pltpu.HBM)
VMEM = pl.BlockSpec(memory_space=pltpu.VMEM)
SMEM = pl.BlockSpec(memory_space=pltpu.SMEM)


def stage_kernel(
    place_ref, counts_ref, cols_ref, amps_hbm, own_ints_ref, left_ref, chunks_hbm, held_ref, total_ref, same_ref, in_sems, out_sems, same_sems
):
    partners, chunk_count, chunk_rows, virtuals = amps_hbm.shape
    aux_count, slot_count, tile, _ = own_ints_ref.shape
    columns = virtuals // tile
    lines = total_ref.shape[0]
    part = (same_ref.shape[0] - lines) // (aux_count * slot_count)

    def load(index):
        return pltpu.make_async_copy(amps_hbm.at[index], held_ref.at[index], in_sems.at[index])

    def store(index, column):
        place = pl.ds((index * columns + column) * chunk_rows, chunk_rows)
        source = held_ref.at[index, :, :, pl.ds(column * tile, tile)]
        return pltpu.make_async_copy(source, chunks_hbm.at[:, place, :], out_sems.at[index, column])

    def send(chunk):
        place = pl.ds(partners * tile, same_ref.shape[0])
        return pltpu.make_async_copy(same_ref, chunks_hbm.at[chunk, place, :], same_sems.at[chunk])

    for index in range(partners):
        load(index).start()

    count = counts_ref[place_ref[0]]
    first = pl.multiple_of(place_ref[1] * part, part)
    for aux in range(aux_count):
        for slot in range(slot_count):
            live = (slot < count).astype(jnp.float32).astype(jnp.bfloat16)
            at = lines + (aux * slot_count + slot) * part
            same_ref[at : at + part, :] = own_ints_ref[aux, slot, pl.ds(first, part), :] * live

    for index in range(partners):
        load(index).wait()
        for column in range(columns):
            store(index, column).start()
        for column in range(columns):
            rows = held_ref[index, :, :, column * tile : (column + 1) * tile].reshape(tile, tile)
            total = jnp.dot(left_ref[...], rows, preferred_element_type=jnp.float32)
            for aux in range(aux_count):
                line = (aux * partners + index) * columns + column
                total_ref[line : line + 1, :] = total[aux : aux + 1]
    same_ref[:lines, :] = total_ref[...].astype(jnp.bfloat16)
    for chunk in range(chunk_count):
        send(chunk).start()
    for index in range(partners):
        for column in range(columns):
            store(index, column).wait()
    for chunk in range(chunk_count):
        send(chunk).wait()


def stage(place, counts, cols, amps, own_ints, left, parts):
    partners, chunk_count, chunk_rows, virtuals = amps.shape
    aux_count, slot_count, tile, _ = own_ints.shape
    columns = virtuals // tile
    lines = aux_count * partners * columns
    same = lines + aux_count * slot_count * tile // parts
    return pl.pallas_call(
        stage_kernel,
        in_specs=[SMEM, SMEM, SMEM, HBM, VMEM, VMEM],
        out_specs=HBM,
        out_shape=jax.ShapeDtypeStruct((chunk_count, partners * tile + same, tile), amps.dtype),
        scratch_shapes=[
            pltpu.VMEM(amps.shape, amps.dtype),
            pltpu.VMEM((lines, tile), jnp.float32),
            pltpu.VMEM((same, tile), amps.dtype),
            pltpu.SemaphoreType.DMA((partners,)),
            pltpu.SemaphoreType.DMA((partners, columns)),
            pltpu.SemaphoreType.DMA((chunk_count,)),
        ],
        compiler_params=pltpu.CompilerParams(vmem_limit_bytes=60 * MIB),
        cost_estimate=pl.CostEstimate(flops=10**7, bytes_accessed=10 * MIB, transcendentals=0),
    )(place, counts, cols, amps, own_ints, left)


def pick_kernel(partners, cols_ref, spread_hbm, out_hbm, shared_hbm, held_ref, sums_ref, shared_ref, in_sems, out_sems, part_sems, sems):
    chunks, slots = in_sems.shape
    lines = sums_ref.shape[1]
    rows = held_ref.shape[1] // slots
    part = spread_hbm.shape[1] - rows - lines

    def fetch(chunk, slot):
        source = spread_hbm.at[cols_ref[slot + 1, chunk], pl.ds(0, rows), :]
        return pltpu.make_async_copy(source, held_ref.at[chunk, pl.ds(slot * rows, rows), :], in_sems.at[chunk, slot])

    def store(chunk):
        return pltpu.make_async_copy(held_ref.at[chunk], out_hbm.at[chunk], out_sems.at[chunk])

    def part_copy(chunk):
        source = spread_hbm.at[chunk, pl.ds(rows + lines, part), :]
        return pltpu.make_async_copy(source, shared_ref.at[pl.ds(chunk * part, part), :], part_sems.at[chunk])

    sums_in = pltpu.make_async_copy(spread_hbm.at[:, pl.ds(rows, lines), :], sums_ref, sems.at[0])
    shared_out = pltpu.make_async_copy(shared_ref, shared_hbm, sems.at[1])
    sums_in.start()
    for chunk in range(chunks):
        part_copy(chunk).start()

    @pl.loop(0, chunks)
    def _(chunk):
        for slot in range(slots):
            fetch(chunk, slot).start()

    sums_in.wait()
    total = jnp.sum(sums_ref[...].astype(jnp.float32), axis=0)
    value = total.astype(jnp.bfloat16)
    shared_ref[chunks * part : chunks * part + lines, :] = value
    shared_ref[chunks * part + lines :, :] = (total - value.astype(jnp.float32)).astype(jnp.bfloat16)
    for chunk in range(chunks):
        part_copy(chunk).wait()
    shared_out.start()

    @pl.loop(0, chunks)
    def _(chunk):
        for slot in range(slots):
            fetch(chunk, slot).wait()
        store(chunk).start()

    @pl.loop(0, chunks)
    def _(chunk):
        store(chunk).wait()

    shared_out.wait()


def pick(partners, lines, spread, cols):
    slots, chunks = cols.shape
    rows, tile = spread.shape[1:]
    part = rows - partners * tile - lines
    shape = (chunks, (slots - 1) * partners * tile, tile)
    shared = (chunks * part + 2 * lines, tile)
    return pl.pallas_call(
        functools.partial(pick_kernel, partners),
        in_specs=[SMEM, HBM],
        out_specs=[HBM, HBM],
        out_shape=[jax.ShapeDtypeStruct(shape, spread.dtype), jax.ShapeDtypeStruct(shared, spread.dtype)],
        scratch_shapes=[
            pltpu.VMEM(shape, spread.dtype),
            pltpu.VMEM((chunks, lines, tile), spread.dtype),
            pltpu.VMEM(shared, spread.dtype),
            pltpu.SemaphoreType.DMA((chunks, slots - 1)),
            pltpu.SemaphoreType.DMA((chunks,)),
            pltpu.SemaphoreType.DMA((chunks,)),
            pltpu.SemaphoreType.DMA((2,)),
        ],
        compiler_params=pltpu.CompilerParams(vmem_limit_bytes=60 * MIB),
        cost_estimate=pl.CostEstimate(flops=0, bytes_accessed=20 * MIB, transcendentals=0),
    )(cols, spread)


def ladder_kernel(cols_ref, counts_ref, place_ref, amps_hbm, fetched_hbm, ints_hbm, own_ints_ref, left_ref, out_hbm, *rest):
    near_ref, far_ref, ints_ref, cycle_ref, sums_ref, own_ref, half_ref, out_ref = rest[:8]
    near_sems, far_sems, int_sems, cycle_sem, out_sems = rest[8:]
    aux_count, slot_count, tile, _ = own_ints_ref.shape
    partners, _, chunk_rows, virtuals = amps_hbm.shape
    tile_count = virtuals // tile
    held = ints_ref.shape[1]
    part_rows = held // tile_count
    part = part_rows // (aux_count * slot_count)
    wide = virtuals // ROW_CHUNKS
    per_chunk = wide // tile
    group = tile_count // INT_CHUNKS
    lines = sums_ref.shape[0]

    def near_copy(partner, chunk):
        span = pl.ds(pl.multiple_of(chunk * wide, wide), wide)
        source = amps_hbm.at[partner, :, :, span]
        return pltpu.make_async_copy(source, near_ref.at[partner, :, :, span], near_sems.at[partner, chunk])

    def far_copy(partner, slot, chunk):
        rows = per_chunk * chunk_rows
        span = pl.ds(pl.multiple_of((slot * partners + partner) * tile + chunk * rows, rows), rows)
        return pltpu.make_async_copy(fetched_hbm.at[:, span, :], far_ref.at[:, span, :], far_sems.at[partner, slot, chunk])

    def int_copy(chunk):
        rows = group * part_rows
        span = pl.ds(pl.multiple_of(chunk * rows, rows), rows)
        return pltpu.make_async_copy(ints_hbm.at[:, span, :], ints_ref.at[:, span, :], int_sems.at[chunk])

    def out_copy(chunk):
        span = pl.ds(pl.multiple_of(chunk * group * tile, group * tile), group * tile)
        return pltpu.make_async_copy(out_ref.at[:, span], out_hbm.at[:, span], out_sems.at[chunk])

    cycle_copy = pltpu.make_async_copy(ints_hbm.at[:, pl.ds(held, 2 * lines), :], cycle_ref, cycle_sem)

    for chunk in range(ROW_CHUNKS):
        for partner in range(partners):
            near_copy(partner, chunk).start()
            for slot in range(slot_count - 1):
                far_copy(partner, slot, chunk).start()
    cycle_copy.start()
    for chunk in range(INT_CHUNKS):
        int_copy(chunk).start()

    count = counts_ref[place_ref[0]]
    for aux in range(aux_count):
        for slot in range(slot_count):
            live = (slot < count).astype(jnp.float32).astype(jnp.bfloat16)
            own_ref[aux * tile : (aux + 1) * tile, slot * tile : (slot + 1) * tile] = own_ints_ref[aux, slot] * live
    line = lax.broadcasted_iota(jnp.int32, (8, tile), 0)
    left = jnp.zeros((8, tile), jnp.float32)
    for aux in range(aux_count):
        left = jnp.where(line == aux, left_ref[aux : aux + 1, :].astype(jnp.float32), left)
    left = left.T

    @pl.loop(0, ROW_CHUNKS)
    def _(chunk):
        for partner in range(partners):
            near_copy(partner, chunk).wait()
            for slot in range(slot_count - 1):
                far_copy(partner, slot, chunk).wait()
        for piece in range(per_chunk):
            column = chunk * per_chunk + piece
            span = pl.ds(pl.multiple_of(column * tile, tile), tile)
            for partner in range(partners):
                rows = [near_ref[partner, :, :, span].reshape(tile, tile)]
                for slot in range(slot_count - 1):
                    first = pl.multiple_of((slot * partners + partner) * tile + column * chunk_rows, chunk_rows)
                    rows.append(far_ref[:, pl.ds(first, chunk_rows), :].reshape(tile, tile))
                total = jnp.dot(own_ref[...], jnp.concatenate(rows), preferred_element_type=jnp.float32).astype(jnp.bfloat16)
                for aux in range(aux_count):
                    half_ref[column, partner * tile : (partner + 1) * tile, aux * tile : (aux + 1) * tile] = total[
                        aux * tile : (aux + 1) * tile
                    ]

    cycle_copy.wait()
    sums = jnp.sum(cycle_ref[...].astype(jnp.float32), axis=0)
    sums_ref[...] = sums[:lines] + sums[lines:]

    @pl.loop(0, INT_CHUNKS)
    def _(chunk):
        int_copy(chunk).wait()
        for piece in range(group):
            row = chunk * group + piece
            halves, ints = [], []
            for slot in range(slot_count):
                halves.append(half_ref[cols_ref[slot, row]])
                for aux in range(aux_count):
                    first = pl.multiple_of(row * part_rows + (aux * slot_count + slot) * part, part)
                    ints.append(ints_ref[:, pl.ds(first, part), :].reshape(tile, tile))
            total = lax.dot_general(
                jnp.concatenate(halves, axis=1),
                jnp.concatenate(ints, axis=1),
                (((1,), (1,)), ((), ())),
                preferred_element_type=jnp.float32,
            )
            span = pl.ds(pl.multiple_of(row * tile, tile), tile)
            for partner in range(partners):
                part_total = total[partner * tile : (partner + 1) * tile]
                for aux in range(aux_count):
                    right = sums_ref[pl.ds((aux * partners + partner) * tile_count + row, 1), :]
                    part_total += left[:, aux : aux + 1] * right
                out_ref[partner * tile : (partner + 1) * tile, span] = part_total.astype(jnp.bfloat16)
        out_copy(chunk).start()

    @pl.loop(0, INT_CHUNKS)
    def _(chunk):
        out_copy(chunk).wait()


def ladder(cols, counts, place, amps, fetched, ints, own_ints, left):
    partners, chunks, chunk_rows, virtuals = amps.shape
    aux_count, slot_count, tile, _ = own_ints.shape
    parts = ints.shape[0]
    tile_count = virtuals // tile
    lines = aux_count * partners * tile_count
    held = ints.shape[1] - 2 * lines
    return pl.pallas_call(
        ladder_kernel,
        in_specs=[SMEM] * 3 + [HBM] * 3 + [VMEM] * 2,
        out_specs=HBM,
        out_shape=jax.ShapeDtypeStruct((partners * tile, virtuals), jnp.bfloat16),
        scratch_shapes=[
            pltpu.VMEM(amps.shape, jnp.bfloat16),
            pltpu.VMEM(fetched.shape, jnp.bfloat16),
            pltpu.VMEM((parts, held, tile), jnp.bfloat16),
            pltpu.VMEM((parts, 2 * lines, tile), jnp.bfloat16),
            pltpu.VMEM((lines, tile), jnp.float32),
            pltpu.VMEM((aux_count * tile, slot_count * tile), jnp.bfloat16),
            pltpu.VMEM((tile_count, partners * tile, aux_count * tile), jnp.bfloat16),
            pltpu.VMEM((partners * tile, virtuals), jnp.bfloat16),
            pltpu.SemaphoreType.DMA((partners, ROW_CHUNKS)),
            pltpu.SemaphoreType.DMA((partners, slot_count - 1, ROW_CHUNKS)),
            pltpu.SemaphoreType.DMA((INT_CHUNKS,)),
            pltpu.SemaphoreType.DMA,
            pltpu.SemaphoreType.DMA((INT_CHUNKS,)),
        ],
        compiler_params=pltpu.CompilerParams(vmem_limit_bytes=60 * MIB),
        cost_estimate=pl.CostEstimate(flops=12 * 10**9, bytes_accessed=30 * MIB, transcendentals=0),
    )(cols, counts, place, amps, fetched, ints, own_ints, left)


def body(amplitudes, ladder_ints, tile_cols, tile_counts, cycle_ints):
    tile_count, slot_count = tile_cols.shape
    aux_count = ladder_ints.shape[0]
    tile = ladder_ints.shape[3]
    partners = amplitudes.shape[1]
    virtuals = amplitudes.shape[3]
    parts = lax.axis_size("occ")
    amps = amplitudes[0].reshape(partners, tile_count, tile // tile_count, virtuals)
    own_ints = ladder_ints[:, 0]
    left = cycle_ints[:, 0, :]
    place = jnp.stack([lax.axis_index("vir"), lax.axis_index("occ")])
    cols = tile_cols.T
    lines = aux_count * partners * tile_count

    chunks = stage(place, tile_counts, cols, amps, own_ints, left, parts)
    spread = lax.all_to_all(chunks, "vir", split_axis=0, concat_axis=0, tiled=True)
    picked, shared = pick(partners, lines, spread, cols)
    ints = lax.all_gather(shared, "occ", axis=0)
    fetched = lax.all_to_all(picked, "vir", split_axis=0, concat_axis=0, tiled=True)
    out = ladder(cols, tile_counts, place, amps, fetched, ints, own_ints, left)
    return out.reshape(1, partners, tile, virtuals)


def solution(mesh):
    in_specs = (
        P("occ", None, "vir", None),
        P(None, "vir", None, None, None),
        P(),
        P(),
        P(None, "occ", "vir"),
    )
    out_specs = P("occ", None, "vir", None)
    return jax.shard_map(body, mesh=mesh, in_specs=in_specs, out_specs=out_specs, check_vma=False)
```

```python
import functools

import jax
import jax.numpy as jnp
from jax import lax
from jax.experimental import pallas as pl
from jax.experimental.pallas import tpu as pltpu
from jax.sharding import PartitionSpec as P

ROW_CHUNKS = 4
INT_CHUNKS = 4
MIB = 2**20
HBM = pl.BlockSpec(memory_space=pltpu.HBM)
VMEM = pl.BlockSpec(memory_space=pltpu.VMEM)
SMEM = pl.BlockSpec(memory_space=pltpu.SMEM)


def stage_kernel(
    place_ref, counts_ref, cols_ref, amps_hbm, own_ints_ref, left_ref, chunks_hbm, held_ref, total_ref, same_ref, in_sems, out_sems, same_sems
):
    partners, chunk_count, chunk_rows, virtuals = amps_hbm.shape
    aux_count, slot_count, tile, _ = own_ints_ref.shape
    columns = virtuals // tile
    lines = total_ref.shape[0]
    part = (same_ref.shape[0] - lines) // (aux_count * slot_count)

    def load(index):
        return pltpu.make_async_copy(amps_hbm.at[index], held_ref.at[index], in_sems.at[index])

    def store(index, column):
        place = pl.ds((index * columns + column) * chunk_rows, chunk_rows)
        source = held_ref.at[index, :, :, pl.ds(column * tile, tile)]
        return pltpu.make_async_copy(source, chunks_hbm.at[:, place, :], out_sems.at[index, column])

    def send(chunk, first, rows, index):
        place = pl.ds(partners * tile + first, rows)
        return pltpu.make_async_copy(same_ref.at[pl.ds(first, rows), :], chunks_hbm.at[chunk, place, :], same_sems.at[index, chunk])

    for index in range(partners):
        load(index).start()

    count = counts_ref[place_ref[0]]
    first = pl.multiple_of(place_ref[1] * part, part)
    for aux in range(aux_count):
        for slot in range(slot_count):
            live = (slot < count).astype(jnp.float32).astype(jnp.bfloat16)
            at = lines + (aux * slot_count + slot) * part
            same_ref[at : at + part, :] = own_ints_ref[aux, slot, pl.ds(first, part), :] * live
    for chunk in range(chunk_count):
        send(chunk, lines, same_ref.shape[0] - lines, 0).start()

    for index in range(partners):
        load(index).wait()
        for column in range(columns):
            store(index, column).start()
        for column in range(columns):
            rows = held_ref[index, :, :, column * tile : (column + 1) * tile].reshape(tile, tile)
            total = jnp.dot(left_ref[...], rows, preferred_element_type=jnp.float32)
            for aux in range(aux_count):
                line = (aux * partners + index) * columns + column
                total_ref[line : line + 1, :] = total[aux : aux + 1]
    same_ref[:lines, :] = total_ref[...].astype(jnp.bfloat16)
    for chunk in range(chunk_count):
        send(chunk, 0, lines, 1).start()
    for index in range(partners):
        for column in range(columns):
            store(index, column).wait()
    for chunk in range(chunk_count):
        send(chunk, lines, same_ref.shape[0] - lines, 0).wait()
        send(chunk, 0, lines, 1).wait()


def stage(place, counts, cols, amps, own_ints, left, parts):
    partners, chunk_count, chunk_rows, virtuals = amps.shape
    aux_count, slot_count, tile, _ = own_ints.shape
    columns = virtuals // tile
    lines = aux_count * partners * columns
    same = lines + aux_count * slot_count * tile // parts
    return pl.pallas_call(
        stage_kernel,
        in_specs=[SMEM, SMEM, SMEM, HBM, VMEM, VMEM],
        out_specs=HBM,
        out_shape=jax.ShapeDtypeStruct((chunk_count, partners * tile + same, tile), amps.dtype),
        scratch_shapes=[
            pltpu.VMEM(amps.shape, amps.dtype),
            pltpu.VMEM((lines, tile), jnp.float32),
            pltpu.VMEM((same, tile), amps.dtype),
            pltpu.SemaphoreType.DMA((partners,)),
            pltpu.SemaphoreType.DMA((partners, columns)),
            pltpu.SemaphoreType.DMA((2, chunk_count)),
        ],
        compiler_params=pltpu.CompilerParams(vmem_limit_bytes=60 * MIB),
        cost_estimate=pl.CostEstimate(flops=10**7, bytes_accessed=10 * MIB, transcendentals=0),
    )(place, counts, cols, amps, own_ints, left)


def pick_kernel(partners, cols_ref, spread_hbm, out_hbm, shared_hbm, held_ref, sums_ref, shared_ref, in_sems, out_sems, part_sems, sems):
    chunks, slots = out_sems.shape
    lines = sums_ref.shape[1]
    rows = held_ref.shape[1]
    part = spread_hbm.shape[1] - rows - lines

    def fetch(chunk):
        return pltpu.make_async_copy(spread_hbm.at[chunk, pl.ds(0, rows), :], held_ref.at[chunk], in_sems.at[chunk])

    def store(chunk, slot):
        place = out_hbm.at[chunk, pl.ds(slot * rows, rows), :]
        return pltpu.make_async_copy(held_ref.at[cols_ref[slot + 1, chunk]], place, out_sems.at[chunk, slot])

    def part_copy(chunk):
        source = spread_hbm.at[chunk, pl.ds(rows + lines, part), :]
        return pltpu.make_async_copy(source, shared_ref.at[pl.ds(chunk * part, part), :], part_sems.at[chunk])

    sums_in = pltpu.make_async_copy(spread_hbm.at[:, pl.ds(rows, lines), :], sums_ref, sems.at[0])
    shared_out = pltpu.make_async_copy(shared_ref, shared_hbm, sems.at[1])
    sums_in.start()
    for chunk in range(chunks):
        fetch(chunk).start()
    for chunk in range(chunks):
        part_copy(chunk).start()

    sums_in.wait()
    total = jnp.sum(sums_ref[...].astype(jnp.float32), axis=0)
    value = total.astype(jnp.bfloat16)
    shared_ref[chunks * part : chunks * part + lines, :] = value
    shared_ref[chunks * part + lines :, :] = (total - value.astype(jnp.float32)).astype(jnp.bfloat16)
    for chunk in range(chunks):
        fetch(chunk).wait()

    @pl.loop(0, chunks)
    def _(chunk):
        for slot in range(slots):
            store(chunk, slot).start()

    for chunk in range(chunks):
        part_copy(chunk).wait()
    shared_out.start()

    @pl.loop(0, chunks)
    def _(chunk):
        for slot in range(slots):
            store(chunk, slot).wait()

    shared_out.wait()


def pick(partners, lines, spread, cols):
    slots, chunks = cols.shape
    rows, tile = spread.shape[1:]
    part = rows - partners * tile - lines
    shape = (chunks, (slots - 1) * partners * tile, tile)
    shared = (chunks * part + 2 * lines, tile)
    return pl.pallas_call(
        functools.partial(pick_kernel, partners),
        in_specs=[SMEM, HBM],
        out_specs=[HBM, HBM],
        out_shape=[jax.ShapeDtypeStruct(shape, spread.dtype), jax.ShapeDtypeStruct(shared, spread.dtype)],
        scratch_shapes=[
            pltpu.VMEM((chunks, partners * tile, tile), spread.dtype),
            pltpu.VMEM((chunks, lines, tile), spread.dtype),
            pltpu.VMEM(shared, spread.dtype),
            pltpu.SemaphoreType.DMA((chunks,)),
            pltpu.SemaphoreType.DMA((chunks, slots - 1)),
            pltpu.SemaphoreType.DMA((chunks,)),
            pltpu.SemaphoreType.DMA((2,)),
        ],
        compiler_params=pltpu.CompilerParams(vmem_limit_bytes=60 * MIB),
        cost_estimate=pl.CostEstimate(flops=0, bytes_accessed=20 * MIB, transcendentals=0),
    )(cols, spread)


def ladder_kernel(cols_ref, counts_ref, place_ref, amps_hbm, fetched_hbm, ints_hbm, own_ints_ref, left_ref, out_hbm, *rest):
    near_ref, far_ref, ints_ref, cycle_ref, sums_ref, own_ref, half_ref, out_ref = rest[:8]
    near_sems, far_sems, int_sems, cycle_sem, out_sems = rest[8:]
    aux_count, slot_count, tile, _ = own_ints_ref.shape
    partners, _, chunk_rows, virtuals = amps_hbm.shape
    tile_count = virtuals // tile
    held = ints_ref.shape[1]
    part_rows = held // tile_count
    part = part_rows // (aux_count * slot_count)
    wide = virtuals // ROW_CHUNKS
    per_chunk = wide // tile
    group = tile_count // INT_CHUNKS
    lines = sums_ref.shape[0]

    def near_copy(partner, chunk):
        span = pl.ds(pl.multiple_of(chunk * wide, wide), wide)
        source = amps_hbm.at[partner, :, :, span]
        return pltpu.make_async_copy(source, near_ref.at[partner, :, :, span], near_sems.at[partner, chunk])

    def far_copy(partner, slot, chunk):
        rows = per_chunk * chunk_rows
        span = pl.ds(pl.multiple_of((slot * partners + partner) * tile + chunk * rows, rows), rows)
        return pltpu.make_async_copy(fetched_hbm.at[:, span, :], far_ref.at[:, span, :], far_sems.at[partner, slot, chunk])

    def int_copy(chunk):
        rows = group * part_rows
        span = pl.ds(pl.multiple_of(chunk * rows, rows), rows)
        return pltpu.make_async_copy(ints_hbm.at[:, span, :], ints_ref.at[:, span, :], int_sems.at[chunk])

    def out_copy(chunk):
        span = pl.ds(pl.multiple_of(chunk * group * tile, group * tile), group * tile)
        return pltpu.make_async_copy(out_ref.at[:, span], out_hbm.at[:, span], out_sems.at[chunk])

    cycle_copy = pltpu.make_async_copy(ints_hbm.at[:, pl.ds(held, 2 * lines), :], cycle_ref, cycle_sem)

    for chunk in range(ROW_CHUNKS):
        for partner in range(partners):
            near_copy(partner, chunk).start()
            for slot in range(slot_count - 1):
                far_copy(partner, slot, chunk).start()
    cycle_copy.start()
    for chunk in range(INT_CHUNKS):
        int_copy(chunk).start()

    count = counts_ref[place_ref[0]]
    for aux in range(aux_count):
        for slot in range(slot_count):
            live = (slot < count).astype(jnp.float32).astype(jnp.bfloat16)
            own_ref[aux * tile : (aux + 1) * tile, slot * tile : (slot + 1) * tile] = own_ints_ref[aux, slot] * live
    line = lax.broadcasted_iota(jnp.int32, (8, tile), 0)
    left = jnp.zeros((8, tile), jnp.float32)
    for aux in range(aux_count):
        left = jnp.where(line == aux, left_ref[aux : aux + 1, :].astype(jnp.float32), left)
    left = left.T

    @pl.loop(0, ROW_CHUNKS)
    def _(chunk):
        for partner in range(partners):
            near_copy(partner, chunk).wait()
            for slot in range(slot_count - 1):
                far_copy(partner, slot, chunk).wait()
        for piece in range(per_chunk):
            column = chunk * per_chunk + piece
            span = pl.ds(pl.multiple_of(column * tile, tile), tile)
            for partner in range(partners):
                rows = [near_ref[partner, :, :, span].reshape(tile, tile)]
                for slot in range(slot_count - 1):
                    first = pl.multiple_of((slot * partners + partner) * tile + column * chunk_rows, chunk_rows)
                    rows.append(far_ref[:, pl.ds(first, chunk_rows), :].reshape(tile, tile))
                total = jnp.dot(own_ref[...], jnp.concatenate(rows), preferred_element_type=jnp.float32).astype(jnp.bfloat16)
                for aux in range(aux_count):
                    half_ref[column, partner * tile : (partner + 1) * tile, aux * tile : (aux + 1) * tile] = total[
                        aux * tile : (aux + 1) * tile
                    ]

    cycle_copy.wait()
    sums = jnp.sum(cycle_ref[...].astype(jnp.float32), axis=0)
    sums_ref[...] = sums[:lines] + sums[lines:]

    @pl.loop(0, INT_CHUNKS)
    def _(chunk):
        int_copy(chunk).wait()
        for piece in range(group):
            row = chunk * group + piece
            halves, ints = [], []
            for slot in range(slot_count):
                halves.append(half_ref[cols_ref[slot, row]])
                for aux in range(aux_count):
                    first = pl.multiple_of(row * part_rows + (aux * slot_count + slot) * part, part)
                    ints.append(ints_ref[:, pl.ds(first, part), :].reshape(tile, tile))
            total = lax.dot_general(
                jnp.concatenate(halves, axis=1),
                jnp.concatenate(ints, axis=1),
                (((1,), (1,)), ((), ())),
                preferred_element_type=jnp.float32,
            )
            span = pl.ds(pl.multiple_of(row * tile, tile), tile)
            for partner in range(partners):
                part_total = total[partner * tile : (partner + 1) * tile]
                for aux in range(aux_count):
                    right = sums_ref[pl.ds((aux * partners + partner) * tile_count + row, 1), :]
                    part_total += left[:, aux : aux + 1] * right
                out_ref[partner * tile : (partner + 1) * tile, span] = part_total.astype(jnp.bfloat16)
        out_copy(chunk).start()

    @pl.loop(0, INT_CHUNKS)
    def _(chunk):
        out_copy(chunk).wait()


def ladder(cols, counts, place, amps, fetched, ints, own_ints, left):
    partners, chunks, chunk_rows, virtuals = amps.shape
    aux_count, slot_count, tile, _ = own_ints.shape
    parts = ints.shape[0]
    tile_count = virtuals // tile
    lines = aux_count * partners * tile_count
    held = ints.shape[1] - 2 * lines
    return pl.pallas_call(
        ladder_kernel,
        in_specs=[SMEM] * 3 + [HBM] * 3 + [VMEM] * 2,
        out_specs=HBM,
        out_shape=jax.ShapeDtypeStruct((partners * tile, virtuals), jnp.bfloat16),
        scratch_shapes=[
            pltpu.VMEM(amps.shape, jnp.bfloat16),
            pltpu.VMEM(fetched.shape, jnp.bfloat16),
            pltpu.VMEM((parts, held, tile), jnp.bfloat16),
            pltpu.VMEM((parts, 2 * lines, tile), jnp.bfloat16),
            pltpu.VMEM((lines, tile), jnp.float32),
            pltpu.VMEM((aux_count * tile, slot_count * tile), jnp.bfloat16),
            pltpu.VMEM((tile_count, partners * tile, aux_count * tile), jnp.bfloat16),
            pltpu.VMEM((partners * tile, virtuals), jnp.bfloat16),
            pltpu.SemaphoreType.DMA((partners, ROW_CHUNKS)),
            pltpu.SemaphoreType.DMA((partners, slot_count - 1, ROW_CHUNKS)),
            pltpu.SemaphoreType.DMA((INT_CHUNKS,)),
            pltpu.SemaphoreType.DMA,
            pltpu.SemaphoreType.DMA((INT_CHUNKS,)),
        ],
        compiler_params=pltpu.CompilerParams(vmem_limit_bytes=60 * MIB),
        cost_estimate=pl.CostEstimate(flops=12 * 10**9, bytes_accessed=30 * MIB, transcendentals=0),
    )(cols, counts, place, amps, fetched, ints, own_ints, left)


def body(amplitudes, ladder_ints, tile_cols, tile_counts, cycle_ints):
    tile_count, slot_count = tile_cols.shape
    aux_count = ladder_ints.shape[0]
    tile = ladder_ints.shape[3]
    partners = amplitudes.shape[1]
    virtuals = amplitudes.shape[3]
    parts = lax.axis_size("occ")
    amps = amplitudes[0].reshape(partners, tile_count, tile // tile_count, virtuals)
    own_ints = ladder_ints[:, 0]
    left = cycle_ints[:, 0, :]
    place = jnp.stack([lax.axis_index("vir"), lax.axis_index("occ")])
    cols = tile_cols.T
    lines = aux_count * partners * tile_count

    chunks = stage(place, tile_counts, cols, amps, own_ints, left, parts)
    spread = lax.all_to_all(chunks, "vir", split_axis=0, concat_axis=0, tiled=True)
    picked, shared = pick(partners, lines, spread, cols)
    ints = lax.all_gather(shared, "occ", axis=0)
    fetched = lax.all_to_all(picked, "vir", split_axis=0, concat_axis=0, tiled=True)
    out = ladder(cols, tile_counts, place, amps, fetched, ints, own_ints, left)
    return out.reshape(1, partners, tile, virtuals)


def solution(mesh):
    in_specs = (
        P("occ", None, "vir", None),
        P(None, "vir", None, None, None),
        P(),
        P(),
        P(None, "occ", "vir"),
    )
    out_specs = P("occ", None, "vir", None)
    return jax.shard_map(body, mesh=mesh, in_specs=in_specs, out_specs=out_specs, check_vma=False)
```

```python
import functools

import jax
import jax.numpy as jnp
from jax import lax
from jax.experimental import pallas as pl
from jax.experimental.pallas import tpu as pltpu
from jax.sharding import PartitionSpec as P

ROW_CHUNKS = 4
INT_CHUNKS = 4
AHEAD = 1
INTS_FROM = 2
INT_STEP = INT_CHUNKS // (ROW_CHUNKS - INTS_FROM)
MIB = 2**20
HBM = pl.BlockSpec(memory_space=pltpu.HBM)
VMEM = pl.BlockSpec(memory_space=pltpu.VMEM)
SMEM = pl.BlockSpec(memory_space=pltpu.SMEM)


def stage_kernel(
    place_ref, counts_ref, cols_ref, amps_hbm, own_ints_ref, left_ref, chunks_hbm, held_ref, total_ref, same_ref, in_sems, out_sems, same_sems
):
    partners, chunk_count, chunk_rows, virtuals = amps_hbm.shape
    aux_count, slot_count, tile, _ = own_ints_ref.shape
    columns = virtuals // tile
    lines = total_ref.shape[0]
    part = (same_ref.shape[0] - lines) // (aux_count * slot_count)

    def load(index):
        return pltpu.make_async_copy(amps_hbm.at[index], held_ref.at[index], in_sems.at[index])

    def store(index, column):
        place = pl.ds((index * columns + column) * chunk_rows, chunk_rows)
        source = held_ref.at[index, :, :, pl.ds(column * tile, tile)]
        return pltpu.make_async_copy(source, chunks_hbm.at[:, place, :], out_sems.at[index, column])

    def send(chunk, first, rows, index):
        place = pl.ds(partners * tile + first, rows)
        return pltpu.make_async_copy(same_ref.at[pl.ds(first, rows), :], chunks_hbm.at[chunk, place, :], same_sems.at[index, chunk])

    for index in range(partners):
        load(index).start()

    count = counts_ref[place_ref[0]]
    first = pl.multiple_of(place_ref[1] * part, part)
    for aux in range(aux_count):
        for slot in range(slot_count):
            live = (slot < count).astype(jnp.float32).astype(jnp.bfloat16)
            at = lines + (aux * slot_count + slot) * part
            same_ref[at : at + part, :] = own_ints_ref[aux, slot, pl.ds(first, part), :] * live
    for chunk in range(chunk_count):
        send(chunk, lines, same_ref.shape[0] - lines, 0).start()

    for index in range(partners):
        load(index).wait()
        for column in range(columns):
            store(index, column).start()
        for column in range(columns):
            rows = held_ref[index, :, :, column * tile : (column + 1) * tile].reshape(tile, tile)
            total = jnp.dot(left_ref[...], rows, preferred_element_type=jnp.float32)
            for aux in range(aux_count):
                line = (aux * partners + index) * columns + column
                total_ref[line : line + 1, :] = total[aux : aux + 1]
    same_ref[:lines, :] = total_ref[...].astype(jnp.bfloat16)
    for chunk in range(chunk_count):
        send(chunk, 0, lines, 1).start()
    for index in range(partners):
        for column in range(columns):
            store(index, column).wait()
    for chunk in range(chunk_count):
        send(chunk, lines, same_ref.shape[0] - lines, 0).wait()
        send(chunk, 0, lines, 1).wait()


def stage(place, counts, cols, amps, own_ints, left, parts):
    partners, chunk_count, chunk_rows, virtuals = amps.shape
    aux_count, slot_count, tile, _ = own_ints.shape
    columns = virtuals // tile
    lines = aux_count * partners * columns
    same = lines + aux_count * slot_count * tile // parts
    return pl.pallas_call(
        stage_kernel,
        in_specs=[SMEM, SMEM, SMEM, HBM, VMEM, VMEM],
        out_specs=HBM,
        out_shape=jax.ShapeDtypeStruct((chunk_count, partners * tile + same, tile), amps.dtype),
        scratch_shapes=[
            pltpu.VMEM(amps.shape, amps.dtype),
            pltpu.VMEM((lines, tile), jnp.float32),
            pltpu.VMEM((same, tile), amps.dtype),
            pltpu.SemaphoreType.DMA((partners,)),
            pltpu.SemaphoreType.DMA((partners, columns)),
            pltpu.SemaphoreType.DMA((2, chunk_count)),
        ],
        compiler_params=pltpu.CompilerParams(vmem_limit_bytes=60 * MIB),
        cost_estimate=pl.CostEstimate(flops=10**7, bytes_accessed=10 * MIB, transcendentals=0),
    )(place, counts, cols, amps, own_ints, left)


def pick_kernel(partners, cols_ref, spread_hbm, out_hbm, shared_hbm, held_ref, sums_ref, shared_ref, in_sems, out_sems, part_sems, sems):
    chunks, slots = out_sems.shape
    lines = sums_ref.shape[1]
    rows = held_ref.shape[1]
    part = spread_hbm.shape[1] - rows - lines

    def fetch(chunk):
        return pltpu.make_async_copy(spread_hbm.at[chunk, pl.ds(0, rows), :], held_ref.at[chunk], in_sems.at[chunk])

    def store(chunk, slot):
        place = out_hbm.at[chunk, pl.ds(slot * rows, rows), :]
        return pltpu.make_async_copy(held_ref.at[cols_ref[slot + 1, chunk]], place, out_sems.at[chunk, slot])

    def part_copy(chunk):
        source = spread_hbm.at[chunk, pl.ds(rows + lines, part), :]
        return pltpu.make_async_copy(source, shared_ref.at[pl.ds(chunk * part, part), :], part_sems.at[chunk])

    sums_in = pltpu.make_async_copy(spread_hbm.at[:, pl.ds(rows, lines), :], sums_ref, sems.at[0])
    shared_out = pltpu.make_async_copy(shared_ref, shared_hbm, sems.at[1])
    sums_in.start()
    for chunk in range(chunks):
        fetch(chunk).start()
    for chunk in range(chunks):
        part_copy(chunk).start()

    sums_in.wait()
    total = jnp.sum(sums_ref[...].astype(jnp.float32), axis=0)
    value = total.astype(jnp.bfloat16)
    shared_ref[chunks * part : chunks * part + lines, :] = value
    shared_ref[chunks * part + lines :, :] = (total - value.astype(jnp.float32)).astype(jnp.bfloat16)
    for chunk in range(chunks):
        fetch(chunk).wait()

    @pl.loop(0, chunks)
    def _(chunk):
        for slot in range(slots):
            store(chunk, slot).start()

    for chunk in range(chunks):
        part_copy(chunk).wait()
    shared_out.start()

    @pl.loop(0, chunks)
    def _(chunk):
        for slot in range(slots):
            store(chunk, slot).wait()

    shared_out.wait()


def pick(partners, lines, spread, cols):
    slots, chunks = cols.shape
    rows, tile = spread.shape[1:]
    part = rows - partners * tile - lines
    shape = (chunks, (slots - 1) * partners * tile, tile)
    shared = (chunks * part + 2 * lines, tile)
    return pl.pallas_call(
        functools.partial(pick_kernel, partners),
        in_specs=[SMEM, HBM],
        out_specs=[HBM, HBM],
        out_shape=[jax.ShapeDtypeStruct(shape, spread.dtype), jax.ShapeDtypeStruct(shared, spread.dtype)],
        scratch_shapes=[
            pltpu.VMEM((chunks, partners * tile, tile), spread.dtype),
            pltpu.VMEM((chunks, lines, tile), spread.dtype),
            pltpu.VMEM(shared, spread.dtype),
            pltpu.SemaphoreType.DMA((chunks,)),
            pltpu.SemaphoreType.DMA((chunks, slots - 1)),
            pltpu.SemaphoreType.DMA((chunks,)),
            pltpu.SemaphoreType.DMA((2,)),
        ],
        compiler_params=pltpu.CompilerParams(vmem_limit_bytes=60 * MIB),
        cost_estimate=pl.CostEstimate(flops=0, bytes_accessed=20 * MIB, transcendentals=0),
    )(cols, spread)


def ladder_kernel(cols_ref, counts_ref, place_ref, amps_hbm, fetched_hbm, ints_hbm, own_ints_ref, left_ref, out_hbm, *rest):
    near_ref, far_ref, ints_ref, cycle_ref, sums_ref, own_ref, half_ref, out_ref = rest[:8]
    near_sems, far_sems, int_sems, cycle_sem, out_sems = rest[8:]
    aux_count, slot_count, tile, _ = own_ints_ref.shape
    partners, _, chunk_rows, virtuals = amps_hbm.shape
    tile_count = virtuals // tile
    held = ints_ref.shape[1]
    part_rows = held // tile_count
    part = part_rows // (aux_count * slot_count)
    wide = virtuals // ROW_CHUNKS
    per_chunk = wide // tile
    group = tile_count // INT_CHUNKS
    lines = sums_ref.shape[0]

    def near_copy(partner, chunk):
        span = pl.ds(pl.multiple_of(chunk * wide, wide), wide)
        source = amps_hbm.at[partner, :, :, span]
        return pltpu.make_async_copy(source, near_ref.at[partner, :, :, span], near_sems.at[partner, chunk])

    def far_copy(partner, slot, chunk):
        rows = per_chunk * chunk_rows
        span = pl.ds(pl.multiple_of((slot * partners + partner) * tile + chunk * rows, rows), rows)
        return pltpu.make_async_copy(fetched_hbm.at[:, span, :], far_ref.at[:, span, :], far_sems.at[partner, slot, chunk])

    def int_copy(chunk):
        rows = group * part_rows
        span = pl.ds(pl.multiple_of(chunk * rows, rows), rows)
        return pltpu.make_async_copy(ints_hbm.at[:, span, :], ints_ref.at[:, span, :], int_sems.at[chunk])

    def out_copy(chunk):
        span = pl.ds(pl.multiple_of(chunk * group * tile, group * tile), group * tile)
        return pltpu.make_async_copy(out_ref.at[:, span], out_hbm.at[:, span], out_sems.at[chunk])

    cycle_copy = pltpu.make_async_copy(ints_hbm.at[:, pl.ds(held, 2 * lines), :], cycle_ref, cycle_sem)

    def start_rows(chunk):
        for partner in range(partners):
            near_copy(partner, chunk).start()
            for slot in range(slot_count - 1):
                far_copy(partner, slot, chunk).start()

    for chunk in range(AHEAD):
        start_rows(chunk)

    count = counts_ref[place_ref[0]]
    for aux in range(aux_count):
        for slot in range(slot_count):
            live = (slot < count).astype(jnp.float32).astype(jnp.bfloat16)
            own_ref[aux * tile : (aux + 1) * tile, slot * tile : (slot + 1) * tile] = own_ints_ref[aux, slot] * live
    line = lax.broadcasted_iota(jnp.int32, (8, tile), 0)
    left = jnp.zeros((8, tile), jnp.float32)
    for aux in range(aux_count):
        left = jnp.where(line == aux, left_ref[aux : aux + 1, :].astype(jnp.float32), left)
    left = left.T

    @pl.loop(0, ROW_CHUNKS)
    def _(chunk):
        for partner in range(partners):
            near_copy(partner, chunk).wait()
            for slot in range(slot_count - 1):
                far_copy(partner, slot, chunk).wait()

        @pl.when(chunk + AHEAD < ROW_CHUNKS)
        def _():
            start_rows(chunk + AHEAD)

        @pl.when(chunk == INTS_FROM)
        def _():
            cycle_copy.start()

        @pl.when(chunk >= INTS_FROM)
        def _():
            for index in range(INT_STEP):
                int_copy((chunk - INTS_FROM) * INT_STEP + index).start()

        for piece in range(per_chunk):
            column = chunk * per_chunk + piece
            span = pl.ds(pl.multiple_of(column * tile, tile), tile)
            for partner in range(partners):
                rows = [near_ref[partner, :, :, span].reshape(tile, tile)]
                for slot in range(slot_count - 1):
                    first = pl.multiple_of((slot * partners + partner) * tile + column * chunk_rows, chunk_rows)
                    rows.append(far_ref[:, pl.ds(first, chunk_rows), :].reshape(tile, tile))
                total = jnp.dot(own_ref[...], jnp.concatenate(rows), preferred_element_type=jnp.float32).astype(jnp.bfloat16)
                for aux in range(aux_count):
                    half_ref[column, partner * tile : (partner + 1) * tile, aux * tile : (aux + 1) * tile] = total[
                        aux * tile : (aux + 1) * tile
                    ]

    cycle_copy.wait()
    sums = jnp.sum(cycle_ref[...].astype(jnp.float32), axis=0)
    sums_ref[...] = sums[:lines] + sums[lines:]

    @pl.loop(0, INT_CHUNKS)
    def _(chunk):
        int_copy(chunk).wait()
        for piece in range(group):
            row = chunk * group + piece
            halves, ints = [], []
            for slot in range(slot_count):
                halves.append(half_ref[cols_ref[slot, row]])
                for aux in range(aux_count):
                    first = pl.multiple_of(row * part_rows + (aux * slot_count + slot) * part, part)
                    ints.append(ints_ref[:, pl.ds(first, part), :].reshape(tile, tile))
            total = lax.dot_general(
                jnp.concatenate(halves, axis=1),
                jnp.concatenate(ints, axis=1),
                (((1,), (1,)), ((), ())),
                preferred_element_type=jnp.float32,
            )
            span = pl.ds(pl.multiple_of(row * tile, tile), tile)
            for partner in range(partners):
                part_total = total[partner * tile : (partner + 1) * tile]
                for aux in range(aux_count):
                    right = sums_ref[pl.ds((aux * partners + partner) * tile_count + row, 1), :]
                    part_total += left[:, aux : aux + 1] * right
                out_ref[partner * tile : (partner + 1) * tile, span] = part_total.astype(jnp.bfloat16)
        out_copy(chunk).start()

    @pl.loop(0, INT_CHUNKS)
    def _(chunk):
        out_copy(chunk).wait()


def ladder(cols, counts, place, amps, fetched, ints, own_ints, left):
    partners, chunks, chunk_rows, virtuals = amps.shape
    aux_count, slot_count, tile, _ = own_ints.shape
    parts = ints.shape[0]
    tile_count = virtuals // tile
    lines = aux_count * partners * tile_count
    held = ints.shape[1] - 2 * lines
    return pl.pallas_call(
        ladder_kernel,
        in_specs=[SMEM] * 3 + [HBM] * 3 + [VMEM] * 2,
        out_specs=HBM,
        out_shape=jax.ShapeDtypeStruct((partners * tile, virtuals), jnp.bfloat16),
        scratch_shapes=[
            pltpu.VMEM(amps.shape, jnp.bfloat16),
            pltpu.VMEM(fetched.shape, jnp.bfloat16),
            pltpu.VMEM((parts, held, tile), jnp.bfloat16),
            pltpu.VMEM((parts, 2 * lines, tile), jnp.bfloat16),
            pltpu.VMEM((lines, tile), jnp.float32),
            pltpu.VMEM((aux_count * tile, slot_count * tile), jnp.bfloat16),
            pltpu.VMEM((tile_count, partners * tile, aux_count * tile), jnp.bfloat16),
            pltpu.VMEM((partners * tile, virtuals), jnp.bfloat16),
            pltpu.SemaphoreType.DMA((partners, ROW_CHUNKS)),
            pltpu.SemaphoreType.DMA((partners, slot_count - 1, ROW_CHUNKS)),
            pltpu.SemaphoreType.DMA((INT_CHUNKS,)),
            pltpu.SemaphoreType.DMA,
            pltpu.SemaphoreType.DMA((INT_CHUNKS,)),
        ],
        compiler_params=pltpu.CompilerParams(vmem_limit_bytes=60 * MIB),
        cost_estimate=pl.CostEstimate(flops=12 * 10**9, bytes_accessed=30 * MIB, transcendentals=0),
    )(cols, counts, place, amps, fetched, ints, own_ints, left)


def body(amplitudes, ladder_ints, tile_cols, tile_counts, cycle_ints):
    tile_count, slot_count = tile_cols.shape
    aux_count = ladder_ints.shape[0]
    tile = ladder_ints.shape[3]
    partners = amplitudes.shape[1]
    virtuals = amplitudes.shape[3]
    parts = lax.axis_size("occ")
    amps = amplitudes[0].reshape(partners, tile_count, tile // tile_count, virtuals)
    own_ints = ladder_ints[:, 0]
    left = cycle_ints[:, 0, :]
    place = jnp.stack([lax.axis_index("vir"), lax.axis_index("occ")])
    cols = tile_cols.T
    lines = aux_count * partners * tile_count

    chunks = stage(place, tile_counts, cols, amps, own_ints, left, parts)
    spread = lax.all_to_all(chunks, "vir", split_axis=0, concat_axis=0, tiled=True)
    picked, shared = pick(partners, lines, spread, cols)
    ints = lax.all_gather(shared, "occ", axis=0)
    fetched = lax.all_to_all(picked, "vir", split_axis=0, concat_axis=0, tiled=True)
    out = ladder(cols, tile_counts, place, amps, fetched, ints, own_ints, left)
    return out.reshape(1, partners, tile, virtuals)


def solution(mesh):
    in_specs = (
        P("occ", None, "vir", None),
        P(None, "vir", None, None, None),
        P(),
        P(),
        P(None, "occ", "vir"),
    )
    out_specs = P("occ", None, "vir", None)
    return jax.shard_map(body, mesh=mesh, in_specs=in_specs, out_specs=out_specs, check_vma=False)
```

```python
import functools

import jax
import jax.numpy as jnp
from jax import lax
from jax.experimental import pallas as pl
from jax.experimental.pallas import tpu as pltpu
from jax.sharding import PartitionSpec as P

LOADS = 4
ROW_CHUNKS = 4
INT_CHUNKS = 4
AHEAD = 1
INTS_FROM = 2
INT_STEP = INT_CHUNKS // (ROW_CHUNKS - INTS_FROM)
MIB = 2**20
HBM = pl.BlockSpec(memory_space=pltpu.HBM)
VMEM = pl.BlockSpec(memory_space=pltpu.VMEM)
SMEM = pl.BlockSpec(memory_space=pltpu.SMEM)


def stage_kernel(
    place_ref, counts_ref, cols_ref, amps_hbm, own_ints_ref, left_ref, chunks_hbm, held_ref, total_ref, same_ref, in_sems, out_sems, same_sems
):
    partners, chunk_count, chunk_rows, virtuals = amps_hbm.shape
    aux_count, slot_count, tile, _ = own_ints_ref.shape
    columns = virtuals // tile
    lines = total_ref.shape[0]
    part = (same_ref.shape[0] - lines) // (aux_count * slot_count)

    pieces = in_sems.shape[1]
    wide = virtuals // pieces

    def load(index, piece):
        span = pl.ds(piece * wide, wide)
        return pltpu.make_async_copy(
            amps_hbm.at[index, :, :, span], held_ref.at[index, :, :, span], in_sems.at[index, piece]
        )

    def store(index, column):
        place = pl.ds((index * columns + column) * chunk_rows, chunk_rows)
        source = held_ref.at[index, :, :, pl.ds(column * tile, tile)]
        return pltpu.make_async_copy(source, chunks_hbm.at[:, place, :], out_sems.at[index, column])

    def send(chunk, first, rows, index):
        place = pl.ds(partners * tile + first, rows)
        return pltpu.make_async_copy(same_ref.at[pl.ds(first, rows), :], chunks_hbm.at[chunk, place, :], same_sems.at[index, chunk])

    for index in range(partners):
        for piece in range(pieces):
            load(index, piece).start()

    count = counts_ref[place_ref[0]]
    first = pl.multiple_of(place_ref[1] * part, part)
    for aux in range(aux_count):
        for slot in range(slot_count):
            live = (slot < count).astype(jnp.float32).astype(jnp.bfloat16)
            at = lines + (aux * slot_count + slot) * part
            same_ref[at : at + part, :] = own_ints_ref[aux, slot, pl.ds(first, part), :] * live
    for chunk in range(chunk_count):
        send(chunk, lines, same_ref.shape[0] - lines, 0).start()

    for index in range(partners):
        for piece in range(pieces):
            load(index, piece).wait()
            for column in range(piece * columns // pieces, (piece + 1) * columns // pieces):
                store(index, column).start()
        for column in range(columns):
            rows = held_ref[index, :, :, column * tile : (column + 1) * tile].reshape(tile, tile)
            total = jnp.dot(left_ref[...], rows, preferred_element_type=jnp.float32)
            for aux in range(aux_count):
                line = (aux * partners + index) * columns + column
                total_ref[line : line + 1, :] = total[aux : aux + 1]
    same_ref[:lines, :] = total_ref[...].astype(jnp.bfloat16)
    for chunk in range(chunk_count):
        send(chunk, 0, lines, 1).start()
    for index in range(partners):
        for column in range(columns):
            store(index, column).wait()
    for chunk in range(chunk_count):
        send(chunk, lines, same_ref.shape[0] - lines, 0).wait()
        send(chunk, 0, lines, 1).wait()


def stage(place, counts, cols, amps, own_ints, left, parts):
    partners, chunk_count, chunk_rows, virtuals = amps.shape
    aux_count, slot_count, tile, _ = own_ints.shape
    columns = virtuals // tile
    lines = aux_count * partners * columns
    same = lines + aux_count * slot_count * tile // parts
    return pl.pallas_call(
        stage_kernel,
        in_specs=[SMEM, SMEM, SMEM, HBM, VMEM, VMEM],
        out_specs=HBM,
        out_shape=jax.ShapeDtypeStruct((chunk_count, partners * tile + same, tile), amps.dtype),
        scratch_shapes=[
            pltpu.VMEM(amps.shape, amps.dtype),
            pltpu.VMEM((lines, tile), jnp.float32),
            pltpu.VMEM((same, tile), amps.dtype),
            pltpu.SemaphoreType.DMA((partners, LOADS)),
            pltpu.SemaphoreType.DMA((partners, columns)),
            pltpu.SemaphoreType.DMA((2, chunk_count)),
        ],
        compiler_params=pltpu.CompilerParams(vmem_limit_bytes=60 * MIB),
        cost_estimate=pl.CostEstimate(flops=10**7, bytes_accessed=10 * MIB, transcendentals=0),
    )(place, counts, cols, amps, own_ints, left)


def pick_kernel(partners, cols_ref, spread_hbm, out_hbm, shared_hbm, held_ref, sums_ref, shared_ref, in_sems, out_sems, part_sems, sems):
    chunks, slots = out_sems.shape
    lines = sums_ref.shape[1]
    rows = held_ref.shape[1]
    part = spread_hbm.shape[1] - rows - lines

    def fetch(chunk):
        return pltpu.make_async_copy(spread_hbm.at[chunk, pl.ds(0, rows), :], held_ref.at[chunk], in_sems.at[chunk])

    def store(chunk, slot):
        place = out_hbm.at[chunk, pl.ds(slot * rows, rows), :]
        return pltpu.make_async_copy(held_ref.at[cols_ref[slot + 1, chunk]], place, out_sems.at[chunk, slot])

    def part_copy(chunk):
        source = spread_hbm.at[chunk, pl.ds(rows + lines, part), :]
        return pltpu.make_async_copy(source, shared_ref.at[pl.ds(chunk * part, part), :], part_sems.at[chunk])

    sums_in = pltpu.make_async_copy(spread_hbm.at[:, pl.ds(rows, lines), :], sums_ref, sems.at[0])
    shared_out = pltpu.make_async_copy(shared_ref, shared_hbm, sems.at[1])
    sums_in.start()
    for chunk in range(chunks):
        fetch(chunk).start()
    for chunk in range(chunks):
        part_copy(chunk).start()

    sums_in.wait()
    total = jnp.sum(sums_ref[...].astype(jnp.float32), axis=0)
    value = total.astype(jnp.bfloat16)
    shared_ref[chunks * part : chunks * part + lines, :] = value
    shared_ref[chunks * part + lines :, :] = (total - value.astype(jnp.float32)).astype(jnp.bfloat16)
    for chunk in range(chunks):
        fetch(chunk).wait()

    @pl.loop(0, chunks)
    def _(chunk):
        for slot in range(slots):
            store(chunk, slot).start()

    for chunk in range(chunks):
        part_copy(chunk).wait()
    shared_out.start()

    @pl.loop(0, chunks)
    def _(chunk):
        for slot in range(slots):
            store(chunk, slot).wait()

    shared_out.wait()


def pick(partners, lines, spread, cols):
    slots, chunks = cols.shape
    rows, tile = spread.shape[1:]
    part = rows - partners * tile - lines
    shape = (chunks, (slots - 1) * partners * tile, tile)
    shared = (chunks * part + 2 * lines, tile)
    return pl.pallas_call(
        functools.partial(pick_kernel, partners),
        in_specs=[SMEM, HBM],
        out_specs=[HBM, HBM],
        out_shape=[jax.ShapeDtypeStruct(shape, spread.dtype), jax.ShapeDtypeStruct(shared, spread.dtype)],
        scratch_shapes=[
            pltpu.VMEM((chunks, partners * tile, tile), spread.dtype),
            pltpu.VMEM((chunks, lines, tile), spread.dtype),
            pltpu.VMEM(shared, spread.dtype),
            pltpu.SemaphoreType.DMA((chunks,)),
            pltpu.SemaphoreType.DMA((chunks, slots - 1)),
            pltpu.SemaphoreType.DMA((chunks,)),
            pltpu.SemaphoreType.DMA((2,)),
        ],
        compiler_params=pltpu.CompilerParams(vmem_limit_bytes=60 * MIB),
        cost_estimate=pl.CostEstimate(flops=0, bytes_accessed=20 * MIB, transcendentals=0),
    )(cols, spread)


def ladder_kernel(cols_ref, counts_ref, place_ref, amps_hbm, fetched_hbm, ints_hbm, own_ints_ref, left_ref, out_hbm, *rest):
    near_ref, far_ref, ints_ref, cycle_ref, sums_ref, own_ref, half_ref, out_ref = rest[:8]
    near_sems, far_sems, int_sems, cycle_sem, out_sems = rest[8:]
    aux_count, slot_count, tile, _ = own_ints_ref.shape
    partners, _, chunk_rows, virtuals = amps_hbm.shape
    tile_count = virtuals // tile
    held = ints_ref.shape[1]
    part_rows = held // tile_count
    part = part_rows // (aux_count * slot_count)
    wide = virtuals // ROW_CHUNKS
    per_chunk = wide // tile
    group = tile_count // INT_CHUNKS
    lines = sums_ref.shape[0]

    def near_copy(partner, chunk):
        span = pl.ds(pl.multiple_of(chunk * wide, wide), wide)
        source = amps_hbm.at[partner, :, :, span]
        return pltpu.make_async_copy(source, near_ref.at[partner, :, :, span], near_sems.at[partner, chunk])

    def far_copy(partner, slot, chunk):
        rows = per_chunk * chunk_rows
        span = pl.ds(pl.multiple_of((slot * partners + partner) * tile + chunk * rows, rows), rows)
        return pltpu.make_async_copy(fetched_hbm.at[:, span, :], far_ref.at[:, span, :], far_sems.at[partner, slot, chunk])

    def int_copy(chunk):
        rows = group * part_rows
        span = pl.ds(pl.multiple_of(chunk * rows, rows), rows)
        return pltpu.make_async_copy(ints_hbm.at[:, span, :], ints_ref.at[:, span, :], int_sems.at[chunk])

    def out_copy(chunk):
        span = pl.ds(pl.multiple_of(chunk * group * tile, group * tile), group * tile)
        return pltpu.make_async_copy(out_ref.at[:, span], out_hbm.at[:, span], out_sems.at[chunk])

    cycle_copy = pltpu.make_async_copy(ints_hbm.at[:, pl.ds(held, 2 * lines), :], cycle_ref, cycle_sem)

    def start_rows(chunk):
        for partner in range(partners):
            near_copy(partner, chunk).start()
            for slot in range(slot_count - 1):
                far_copy(partner, slot, chunk).start()

    for chunk in range(AHEAD):
        start_rows(chunk)

    count = counts_ref[place_ref[0]]
    for aux in range(aux_count):
        for slot in range(slot_count):
            live = (slot < count).astype(jnp.float32).astype(jnp.bfloat16)
            own_ref[aux * tile : (aux + 1) * tile, slot * tile : (slot + 1) * tile] = own_ints_ref[aux, slot] * live
    line = lax.broadcasted_iota(jnp.int32, (8, tile), 0)
    left = jnp.zeros((8, tile), jnp.float32)
    for aux in range(aux_count):
        left = jnp.where(line == aux, left_ref[aux : aux + 1, :].astype(jnp.float32), left)
    left = left.T

    @pl.loop(0, ROW_CHUNKS)
    def _(chunk):
        for partner in range(partners):
            near_copy(partner, chunk).wait()
            for slot in range(slot_count - 1):
                far_copy(partner, slot, chunk).wait()

        @pl.when(chunk + AHEAD < ROW_CHUNKS)
        def _():
            start_rows(chunk + AHEAD)

        @pl.when(chunk == INTS_FROM)
        def _():
            cycle_copy.start()

        @pl.when(chunk >= INTS_FROM)
        def _():
            for index in range(INT_STEP):
                int_copy((chunk - INTS_FROM) * INT_STEP + index).start()

        for piece in range(per_chunk):
            column = chunk * per_chunk + piece
            span = pl.ds(pl.multiple_of(column * tile, tile), tile)
            for partner in range(partners):
                rows = [near_ref[partner, :, :, span].reshape(tile, tile)]
                for slot in range(slot_count - 1):
                    first = pl.multiple_of((slot * partners + partner) * tile + column * chunk_rows, chunk_rows)
                    rows.append(far_ref[:, pl.ds(first, chunk_rows), :].reshape(tile, tile))
                total = jnp.dot(own_ref[...], jnp.concatenate(rows), preferred_element_type=jnp.float32).astype(jnp.bfloat16)
                for aux in range(aux_count):
                    half_ref[column, partner * tile : (partner + 1) * tile, aux * tile : (aux + 1) * tile] = total[
                        aux * tile : (aux + 1) * tile
                    ]

    cycle_copy.wait()
    sums = jnp.sum(cycle_ref[...].astype(jnp.float32), axis=0)
    sums_ref[...] = sums[:lines] + sums[lines:]

    @pl.loop(0, INT_CHUNKS)
    def _(chunk):
        int_copy(chunk).wait()
        for piece in range(group):
            row = chunk * group + piece
            halves, ints = [], []
            for slot in range(slot_count):
                halves.append(half_ref[cols_ref[slot, row]])
                for aux in range(aux_count):
                    first = pl.multiple_of(row * part_rows + (aux * slot_count + slot) * part, part)
                    ints.append(ints_ref[:, pl.ds(first, part), :].reshape(tile, tile))
            total = lax.dot_general(
                jnp.concatenate(halves, axis=1),
                jnp.concatenate(ints, axis=1),
                (((1,), (1,)), ((), ())),
                preferred_element_type=jnp.float32,
            )
            span = pl.ds(pl.multiple_of(row * tile, tile), tile)
            for partner in range(partners):
                part_total = total[partner * tile : (partner + 1) * tile]
                for aux in range(aux_count):
                    right = sums_ref[pl.ds((aux * partners + partner) * tile_count + row, 1), :]
                    part_total += left[:, aux : aux + 1] * right
                out_ref[partner * tile : (partner + 1) * tile, span] = part_total.astype(jnp.bfloat16)
        out_copy(chunk).start()

    @pl.loop(0, INT_CHUNKS)
    def _(chunk):
        out_copy(chunk).wait()


def ladder(cols, counts, place, amps, fetched, ints, own_ints, left):
    partners, chunks, chunk_rows, virtuals = amps.shape
    aux_count, slot_count, tile, _ = own_ints.shape
    parts = ints.shape[0]
    tile_count = virtuals // tile
    lines = aux_count * partners * tile_count
    held = ints.shape[1] - 2 * lines
    return pl.pallas_call(
        ladder_kernel,
        in_specs=[SMEM] * 3 + [HBM] * 3 + [VMEM] * 2,
        out_specs=HBM,
        out_shape=jax.ShapeDtypeStruct((partners * tile, virtuals), jnp.bfloat16),
        scratch_shapes=[
            pltpu.VMEM(amps.shape, jnp.bfloat16),
            pltpu.VMEM(fetched.shape, jnp.bfloat16),
            pltpu.VMEM((parts, held, tile), jnp.bfloat16),
            pltpu.VMEM((parts, 2 * lines, tile), jnp.bfloat16),
            pltpu.VMEM((lines, tile), jnp.float32),
            pltpu.VMEM((aux_count * tile, slot_count * tile), jnp.bfloat16),
            pltpu.VMEM((tile_count, partners * tile, aux_count * tile), jnp.bfloat16),
            pltpu.VMEM((partners * tile, virtuals), jnp.bfloat16),
            pltpu.SemaphoreType.DMA((partners, ROW_CHUNKS)),
            pltpu.SemaphoreType.DMA((partners, slot_count - 1, ROW_CHUNKS)),
            pltpu.SemaphoreType.DMA((INT_CHUNKS,)),
            pltpu.SemaphoreType.DMA,
            pltpu.SemaphoreType.DMA((INT_CHUNKS,)),
        ],
        compiler_params=pltpu.CompilerParams(vmem_limit_bytes=60 * MIB),
        cost_estimate=pl.CostEstimate(flops=12 * 10**9, bytes_accessed=30 * MIB, transcendentals=0),
    )(cols, counts, place, amps, fetched, ints, own_ints, left)


def body(amplitudes, ladder_ints, tile_cols, tile_counts, cycle_ints):
    tile_count, slot_count = tile_cols.shape
    aux_count = ladder_ints.shape[0]
    tile = ladder_ints.shape[3]
    partners = amplitudes.shape[1]
    virtuals = amplitudes.shape[3]
    parts = lax.axis_size("occ")
    amps = amplitudes[0].reshape(partners, tile_count, tile // tile_count, virtuals)
    own_ints = ladder_ints[:, 0]
    left = cycle_ints[:, 0, :]
    place = jnp.stack([lax.axis_index("vir"), lax.axis_index("occ")])
    cols = tile_cols.T
    lines = aux_count * partners * tile_count

    chunks = stage(place, tile_counts, cols, amps, own_ints, left, parts)
    spread = lax.all_to_all(chunks, "vir", split_axis=0, concat_axis=0, tiled=True)
    picked, shared = pick(partners, lines, spread, cols)
    ints = lax.all_gather(shared, "occ", axis=0)
    fetched = lax.all_to_all(picked, "vir", split_axis=0, concat_axis=0, tiled=True)
    out = ladder(cols, tile_counts, place, amps, fetched, ints, own_ints, left)
    return out.reshape(1, partners, tile, virtuals)


def solution(mesh):
    in_specs = (
        P("occ", None, "vir", None),
        P(None, "vir", None, None, None),
        P(),
        P(),
        P(None, "occ", "vir"),
    )
    out_specs = P("occ", None, "vir", None)
    return jax.shard_map(body, mesh=mesh, in_specs=in_specs, out_specs=out_specs, check_vma=False)
```

```python
import functools

import jax
import jax.numpy as jnp
from jax import lax
from jax.experimental import pallas as pl
from jax.experimental.pallas import tpu as pltpu
from jax.sharding import PartitionSpec as P

ROW_CHUNKS = 4
INT_CHUNKS = 4
AHEAD = 1
INTS_FROM = 2
INT_STEP = INT_CHUNKS // (ROW_CHUNKS - INTS_FROM)
MIB = 2**20
HBM = pl.BlockSpec(memory_space=pltpu.HBM)
VMEM = pl.BlockSpec(memory_space=pltpu.VMEM)
SMEM = pl.BlockSpec(memory_space=pltpu.SMEM)


def stage_kernel(
    place_ref, counts_ref, cols_ref, amps_hbm, own_ints_ref, left_ref, chunks_hbm, held_ref, total_ref, same_ref, in_sems, out_sems, same_sems
):
    partners, chunk_count, chunk_rows, virtuals = amps_hbm.shape
    aux_count, slot_count, tile, _ = own_ints_ref.shape
    columns = virtuals // tile
    lines = total_ref.shape[0]
    part = (same_ref.shape[0] - lines) // (aux_count * slot_count)

    def load(index):
        return pltpu.make_async_copy(amps_hbm.at[index], held_ref.at[index], in_sems.at[index])

    def store(index, column):
        place = pl.ds((index * columns + column) * chunk_rows, chunk_rows)
        source = held_ref.at[index, :, :, pl.ds(column * tile, tile)]
        return pltpu.make_async_copy(source, chunks_hbm.at[:, place, :], out_sems.at[index, column])

    def send(chunk, first, rows, index):
        place = pl.ds(partners * tile + first, rows)
        return pltpu.make_async_copy(same_ref.at[pl.ds(first, rows), :], chunks_hbm.at[chunk, place, :], same_sems.at[index, chunk])

    for index in range(partners):
        load(index).start()

    count = counts_ref[place_ref[0]]
    first = pl.multiple_of(place_ref[1] * part, part)
    for aux in range(aux_count):
        for slot in range(slot_count):
            live = (slot < count).astype(jnp.float32).astype(jnp.bfloat16)
            at = lines + (aux * slot_count + slot) * part
            same_ref[at : at + part, :] = own_ints_ref[aux, slot, pl.ds(first, part), :] * live
    for chunk in range(chunk_count):
        send(chunk, lines, same_ref.shape[0] - lines, 0).start()

    for index in range(partners):
        load(index).wait()
        for column in range(columns):
            store(index, column).start()
        for column in range(columns):
            rows = held_ref[index, :, :, column * tile : (column + 1) * tile].reshape(tile, tile)
            total = jnp.dot(left_ref[...], rows, preferred_element_type=jnp.float32)
            for aux in range(aux_count):
                line = (aux * partners + index) * columns + column
                total_ref[line : line + 1, :] = total[aux : aux + 1]
    same_ref[:lines, :] = total_ref[...].astype(jnp.bfloat16)
    for chunk in range(chunk_count):
        send(chunk, 0, lines, 1).start()
    for index in range(partners):
        for column in range(columns):
            store(index, column).wait()
    for chunk in range(chunk_count):
        send(chunk, lines, same_ref.shape[0] - lines, 0).wait()
        send(chunk, 0, lines, 1).wait()


def stage(place, counts, cols, amps, own_ints, left, parts):
    partners, chunk_count, chunk_rows, virtuals = amps.shape
    aux_count, slot_count, tile, _ = own_ints.shape
    columns = virtuals // tile
    lines = aux_count * partners * columns
    same = lines + aux_count * slot_count * tile // parts
    return pl.pallas_call(
        stage_kernel,
        in_specs=[SMEM, SMEM, SMEM, HBM, VMEM, VMEM],
        out_specs=HBM,
        out_shape=jax.ShapeDtypeStruct((chunk_count, partners * tile + same, tile), amps.dtype),
        scratch_shapes=[
            pltpu.VMEM(amps.shape, amps.dtype),
            pltpu.VMEM((lines, tile), jnp.float32),
            pltpu.VMEM((same, tile), amps.dtype),
            pltpu.SemaphoreType.DMA((partners,)),
            pltpu.SemaphoreType.DMA((partners, columns)),
            pltpu.SemaphoreType.DMA((2, chunk_count)),
        ],
        compiler_params=pltpu.CompilerParams(vmem_limit_bytes=60 * MIB),
        cost_estimate=pl.CostEstimate(flops=10**7, bytes_accessed=10 * MIB, transcendentals=0),
    )(place, counts, cols, amps, own_ints, left)


def pick_kernel(partners, cols_ref, spread_hbm, out_hbm, shared_hbm, held_ref, sums_ref, shared_ref, in_sems, out_sems, part_sems, sems):
    chunks, slots = out_sems.shape
    lines = sums_ref.shape[1]
    rows = held_ref.shape[1]
    part = spread_hbm.shape[1] - rows - lines

    def fetch(chunk):
        return pltpu.make_async_copy(spread_hbm.at[chunk, pl.ds(0, rows), :], held_ref.at[chunk], in_sems.at[chunk])

    def store(chunk, slot):
        place = out_hbm.at[chunk, pl.ds(slot * rows, rows), :]
        return pltpu.make_async_copy(held_ref.at[cols_ref[slot + 1, chunk]], place, out_sems.at[chunk, slot])

    def part_copy(chunk):
        source = spread_hbm.at[chunk, pl.ds(rows + lines, part), :]
        return pltpu.make_async_copy(source, shared_ref.at[pl.ds(chunk * part, part), :], part_sems.at[chunk])

    sums_in = pltpu.make_async_copy(spread_hbm.at[:, pl.ds(rows, lines), :], sums_ref, sems.at[0])
    shared_out = pltpu.make_async_copy(shared_ref, shared_hbm, sems.at[1])
    sums_in.start()
    for chunk in range(chunks):
        fetch(chunk).start()

    sums_in.wait()
    total = jnp.sum(sums_ref[...].astype(jnp.float32), axis=0)
    value = total.astype(jnp.bfloat16)
    shared_ref[chunks * part : chunks * part + lines, :] = value
    shared_ref[chunks * part + lines :, :] = (total - value.astype(jnp.float32)).astype(jnp.bfloat16)
    for chunk in range(chunks):
        fetch(chunk).wait()

    for chunk in range(chunks):
        part_copy(chunk).start()

    @pl.loop(0, chunks)
    def _(chunk):
        for slot in range(slots):
            store(chunk, slot).start()

    for chunk in range(chunks):
        part_copy(chunk).wait()
    shared_out.start()

    @pl.loop(0, chunks)
    def _(chunk):
        for slot in range(slots):
            store(chunk, slot).wait()

    shared_out.wait()


def pick(partners, lines, spread, cols):
    slots, chunks = cols.shape
    rows, tile = spread.shape[1:]
    part = rows - partners * tile - lines
    shape = (chunks, (slots - 1) * partners * tile, tile)
    shared = (chunks * part + 2 * lines, tile)
    return pl.pallas_call(
        functools.partial(pick_kernel, partners),
        in_specs=[SMEM, HBM],
        out_specs=[HBM, HBM],
        out_shape=[jax.ShapeDtypeStruct(shape, spread.dtype), jax.ShapeDtypeStruct(shared, spread.dtype)],
        scratch_shapes=[
            pltpu.VMEM((chunks, partners * tile, tile), spread.dtype),
            pltpu.VMEM((chunks, lines, tile), spread.dtype),
            pltpu.VMEM(shared, spread.dtype),
            pltpu.SemaphoreType.DMA((chunks,)),
            pltpu.SemaphoreType.DMA((chunks, slots - 1)),
            pltpu.SemaphoreType.DMA((chunks,)),
            pltpu.SemaphoreType.DMA((2,)),
        ],
        compiler_params=pltpu.CompilerParams(vmem_limit_bytes=60 * MIB),
        cost_estimate=pl.CostEstimate(flops=0, bytes_accessed=20 * MIB, transcendentals=0),
    )(cols, spread)


def ladder_kernel(cols_ref, counts_ref, place_ref, amps_hbm, fetched_hbm, ints_hbm, own_ints_ref, left_ref, out_hbm, *rest):
    near_ref, far_ref, ints_ref, cycle_ref, sums_ref, own_ref, half_ref, out_ref = rest[:8]
    near_sems, far_sems, int_sems, cycle_sem, out_sems = rest[8:]
    aux_count, slot_count, tile, _ = own_ints_ref.shape
    partners, _, chunk_rows, virtuals = amps_hbm.shape
    tile_count = virtuals // tile
    held = ints_ref.shape[1]
    part_rows = held // tile_count
    part = part_rows // (aux_count * slot_count)
    wide = virtuals // ROW_CHUNKS
    per_chunk = wide // tile
    group = tile_count // INT_CHUNKS
    lines = sums_ref.shape[0]

    def near_copy(partner, chunk):
        span = pl.ds(pl.multiple_of(chunk * wide, wide), wide)
        source = amps_hbm.at[partner, :, :, span]
        return pltpu.make_async_copy(source, near_ref.at[partner, :, :, span], near_sems.at[partner, chunk])

    def far_copy(partner, slot, chunk):
        rows = per_chunk * chunk_rows
        span = pl.ds(pl.multiple_of((slot * partners + partner) * tile + chunk * rows, rows), rows)
        return pltpu.make_async_copy(fetched_hbm.at[:, span, :], far_ref.at[:, span, :], far_sems.at[partner, slot, chunk])

    def int_copy(chunk):
        rows = group * part_rows
        span = pl.ds(pl.multiple_of(chunk * rows, rows), rows)
        return pltpu.make_async_copy(ints_hbm.at[:, span, :], ints_ref.at[:, span, :], int_sems.at[chunk])

    def out_copy(chunk):
        span = pl.ds(pl.multiple_of(chunk * group * tile, group * tile), group * tile)
        return pltpu.make_async_copy(out_ref.at[:, span], out_hbm.at[:, span], out_sems.at[chunk])

    cycle_copy = pltpu.make_async_copy(ints_hbm.at[:, pl.ds(held, 2 * lines), :], cycle_ref, cycle_sem)

    def start_rows(chunk):
        for partner in range(partners):
            near_copy(partner, chunk).start()
            for slot in range(slot_count - 1):
                far_copy(partner, slot, chunk).start()

    for chunk in range(AHEAD):
        start_rows(chunk)

    count = counts_ref[place_ref[0]]
    for aux in range(aux_count):
        for slot in range(slot_count):
            live = (slot < count).astype(jnp.float32).astype(jnp.bfloat16)
            own_ref[aux * tile : (aux + 1) * tile, slot * tile : (slot + 1) * tile] = own_ints_ref[aux, slot] * live
    line = lax.broadcasted_iota(jnp.int32, (8, tile), 0)
    left = jnp.zeros((8, tile), jnp.float32)
    for aux in range(aux_count):
        left = jnp.where(line == aux, left_ref[aux : aux + 1, :].astype(jnp.float32), left)
    left = left.T

    @pl.loop(0, ROW_CHUNKS)
    def _(chunk):
        for partner in range(partners):
            near_copy(partner, chunk).wait()
            for slot in range(slot_count - 1):
                far_copy(partner, slot, chunk).wait()

        @pl.when(chunk + AHEAD < ROW_CHUNKS)
        def _():
            start_rows(chunk + AHEAD)

        @pl.when(chunk == INTS_FROM)
        def _():
            cycle_copy.start()

        @pl.when(chunk >= INTS_FROM)
        def _():
            for index in range(INT_STEP):
                int_copy((chunk - INTS_FROM) * INT_STEP + index).start()

        for piece in range(per_chunk):
            column = chunk * per_chunk + piece
            span = pl.ds(pl.multiple_of(column * tile, tile), tile)
            for partner in range(partners):
                rows = [near_ref[partner, :, :, span].reshape(tile, tile)]
                for slot in range(slot_count - 1):
                    first = pl.multiple_of((slot * partners + partner) * tile + column * chunk_rows, chunk_rows)
                    rows.append(far_ref[:, pl.ds(first, chunk_rows), :].reshape(tile, tile))
                total = jnp.dot(own_ref[...], jnp.concatenate(rows), preferred_element_type=jnp.float32).astype(jnp.bfloat16)
                for aux in range(aux_count):
                    half_ref[column, partner * tile : (partner + 1) * tile, aux * tile : (aux + 1) * tile] = total[
                        aux * tile : (aux + 1) * tile
                    ]

    cycle_copy.wait()
    sums = jnp.sum(cycle_ref[...].astype(jnp.float32), axis=0)
    sums_ref[...] = sums[:lines] + sums[lines:]

    @pl.loop(0, INT_CHUNKS)
    def _(chunk):
        int_copy(chunk).wait()
        for piece in range(group):
            row = chunk * group + piece
            halves, ints = [], []
            for slot in range(slot_count):
                halves.append(half_ref[cols_ref[slot, row]])
                for aux in range(aux_count):
                    first = pl.multiple_of(row * part_rows + (aux * slot_count + slot) * part, part)
                    ints.append(ints_ref[:, pl.ds(first, part), :].reshape(tile, tile))
            total = lax.dot_general(
                jnp.concatenate(halves, axis=1),
                jnp.concatenate(ints, axis=1),
                (((1,), (1,)), ((), ())),
                preferred_element_type=jnp.float32,
            )
            span = pl.ds(pl.multiple_of(row * tile, tile), tile)
            for partner in range(partners):
                part_total = total[partner * tile : (partner + 1) * tile]
                for aux in range(aux_count):
                    right = sums_ref[pl.ds((aux * partners + partner) * tile_count + row, 1), :]
                    part_total += left[:, aux : aux + 1] * right
                out_ref[partner * tile : (partner + 1) * tile, span] = part_total.astype(jnp.bfloat16)
        out_copy(chunk).start()

    @pl.loop(0, INT_CHUNKS)
    def _(chunk):
        out_copy(chunk).wait()


def ladder(cols, counts, place, amps, fetched, ints, own_ints, left):
    partners, chunks, chunk_rows, virtuals = amps.shape
    aux_count, slot_count, tile, _ = own_ints.shape
    parts = ints.shape[0]
    tile_count = virtuals // tile
    lines = aux_count * partners * tile_count
    held = ints.shape[1] - 2 * lines
    return pl.pallas_call(
        ladder_kernel,
        in_specs=[SMEM] * 3 + [HBM] * 3 + [VMEM] * 2,
        out_specs=HBM,
        out_shape=jax.ShapeDtypeStruct((partners * tile, virtuals), jnp.bfloat16),
        scratch_shapes=[
            pltpu.VMEM(amps.shape, jnp.bfloat16),
            pltpu.VMEM(fetched.shape, jnp.bfloat16),
            pltpu.VMEM((parts, held, tile), jnp.bfloat16),
            pltpu.VMEM((parts, 2 * lines, tile), jnp.bfloat16),
            pltpu.VMEM((lines, tile), jnp.float32),
            pltpu.VMEM((aux_count * tile, slot_count * tile), jnp.bfloat16),
            pltpu.VMEM((tile_count, partners * tile, aux_count * tile), jnp.bfloat16),
            pltpu.VMEM((partners * tile, virtuals), jnp.bfloat16),
            pltpu.SemaphoreType.DMA((partners, ROW_CHUNKS)),
            pltpu.SemaphoreType.DMA((partners, slot_count - 1, ROW_CHUNKS)),
            pltpu.SemaphoreType.DMA((INT_CHUNKS,)),
            pltpu.SemaphoreType.DMA,
            pltpu.SemaphoreType.DMA((INT_CHUNKS,)),
        ],
        compiler_params=pltpu.CompilerParams(vmem_limit_bytes=60 * MIB),
        cost_estimate=pl.CostEstimate(flops=12 * 10**9, bytes_accessed=30 * MIB, transcendentals=0),
    )(cols, counts, place, amps, fetched, ints, own_ints, left)


def body(amplitudes, ladder_ints, tile_cols, tile_counts, cycle_ints):
    tile_count, slot_count = tile_cols.shape
    aux_count = ladder_ints.shape[0]
    tile = ladder_ints.shape[3]
    partners = amplitudes.shape[1]
    virtuals = amplitudes.shape[3]
    parts = lax.axis_size("occ")
    amps = amplitudes[0].reshape(partners, tile_count, tile // tile_count, virtuals)
    own_ints = ladder_ints[:, 0]
    left = cycle_ints[:, 0, :]
    place = jnp.stack([lax.axis_index("vir"), lax.axis_index("occ")])
    cols = tile_cols.T
    lines = aux_count * partners * tile_count

    chunks = stage(place, tile_counts, cols, amps, own_ints, left, parts)
    spread = lax.all_to_all(chunks, "vir", split_axis=0, concat_axis=0, tiled=True)
    picked, shared = pick(partners, lines, spread, cols)
    ints = lax.all_gather(shared, "occ", axis=0)
    fetched = lax.all_to_all(picked, "vir", split_axis=0, concat_axis=0, tiled=True)
    out = ladder(cols, tile_counts, place, amps, fetched, ints, own_ints, left)
    return out.reshape(1, partners, tile, virtuals)


def solution(mesh):
    in_specs = (
        P("occ", None, "vir", None),
        P(None, "vir", None, None, None),
        P(),
        P(),
        P(None, "occ", "vir"),
    )
    out_specs = P("occ", None, "vir", None)
    return jax.shard_map(body, mesh=mesh, in_specs=in_specs, out_specs=out_specs, check_vma=False)
```
